32 devices in a mesh: dp: 16 (over z, y, core), cout: 2 (over x).
Axes of the slice: x: 2, y: 2, z: 4, core: 2. Of those that a mesh axis runs over, the one named last changes fastest.
Arguments:
- images: bfloat16 [64, 512, 1024], P('dp', 'cout'), may hold values from -6 to 6
- styles: float32 [64, 512], P('dp'), may hold values from -5 to 5
- weight: bfloat16 [9, 512, 512], P(None, 'cout', 'dp'), may hold values from -0.09375 to 0.09375
- cotangent: bfloat16 [64, 512, 1024], P('dp', 'cout'), may hold values from -6 to 6
Outputs:
- output: bfloat16 [64, 512, 1024], P('dp', 'cout')
- input_grad: bfloat16 [64, 512, 1024], P('dp', 'cout')
- style_grad: float32 [64, 512], P('dp', 'cout')
- weight_grad: float32 [9, 512, 512], P(None, 'cout', 'dp')
The draws below stay inside these ranges and needn't reach their ends.
All inputs are finite; a program needn't handle non-finite values.
Results may differ from the reference program's by a relative error of at most 0.013.
Values may be sent and summed in bfloat16 or wider, within the bound.
A program may use at most 192 MiB of HBM per device.

```python
import jax
import jax.numpy as jnp
from jax import lax

CIN = 512
COUT = 512
RES = 32
TAPS = 9
BATCH = 64
PIXELS = 1024
N_COUT = 2


def with_spikes(result, stream_key, source, target, shards_of, factor):
    owner, partner = [(jnp.arange(result.shape[dim]) // (result.shape[dim] // shards_of)).reshape([-1 if axis == dim else 1 for axis in range(result.ndim)]) for dim in (source, target)]
    chosen = jax.random.permutation(stream_key, shards_of)[partner]
    strong = (owner == chosen) | (owner == (partner + shards_of // 2) % shards_of)
    return jnp.where(strong, factor * result, result)


def levels(key, extent, split, smallest, largest):
    def one(axis_at, blocks):
        draws = jax.random.uniform(jax.random.fold_in(jax.random.fold_in(key, 6), axis_at), (blocks,), jnp.float32, smallest / len(split), largest / len(split))
        return jnp.repeat(jnp.exp(draws), extent[axis_at] // blocks).reshape((-1,) + (1,) * (len(extent) - axis_at - 1))

    factor_of = one(*split[0])
    for cut in split[1:]:
        factor_of = factor_of * one(*cut)
    return factor_of


def scatter_about(stream_key, extent, spread, limit, pieces=(), kind=jnp.bfloat16):
    gain = levels(stream_key, extent, pieces, -0.22, 0.18) if pieces else 1.0
    result = jax.random.normal(stream_key, extent, jnp.float32) * spread * gain
    return jnp.minimum(jnp.maximum(result, -limit), limit).astype(kind)


def gaussian_with(stream_key, dims, width, most, cuts, heavy, dtype=jnp.bfloat16):
    result = width * jax.random.normal(stream_key, dims, jnp.float32)
    if cuts:
        result = result * levels(stream_key, dims, cuts, -0.22, 0.18)
    return jnp.clip(with_spikes(result, jax.random.fold_in(stream_key, 3), *heavy), -most, most).astype(dtype)


def setup_inputs(seed: int = 0) -> dict:
    key_list = jax.random.split(jax.random.key(seed), 5)
    return {
        "images": gaussian_with(key_list[0], (BATCH, CIN, PIXELS), 1.0, 6.0, ((0, 16), (1, 2)), (0, 1, 16, 2.0)),
        "styles": scatter_about(key_list[1], (BATCH, CIN), 1.0, 5.0, ((0, 16),), jnp.float32),
        "weight": scatter_about(key_list[2], (TAPS, COUT, CIN), (CIN * TAPS) ** -0.5, 0.09375, ((1, 2), (2, 16))),
        "cotangent": scatter_about(key_list[3], (BATCH, COUT, PIXELS), 1.0, 6.0, ((0, 16), (1, 2))),
    }


epsilon = 1e-08
tap_steps = [(-1, -1), (-1, 0), (-1, 1), (0, -1), (0, 0), (0, 1), (1, -1), (1, 0), (1, 1)]

def displace(source, row_step, col_step, grid_side):
    length = source.shape[-1]
    margin = grid_side + 1
    offset = row_step * grid_side + col_step
    widths = [(0, 0)] * (source.ndim - 1) + [(margin, margin)]
    padded = jnp.pad(source, widths)
    moved = lax.slice_in_dim(padded, margin + offset, margin + offset + length, axis=source.ndim - 1)
    column = jnp.arange(length) % grid_side + col_step
    inside = (column >= 0) & (column < grid_side)
    return jnp.where(inside, moved, jnp.zeros_like(moved))

def round_trip(values):
    return lax.optimization_barrier(values.astype(jnp.bfloat16)).astype(jnp.float32)

def reference(images, styles, weight, cotangent):
    kernel_energy = lax.optimization_barrier(jnp.sum(jnp.square(weight.astype(jnp.float32)), axis=0))
    group = COUT // N_COUT
    length = RES * RES

    def step(carry, inputs):
        image, style, upstream = inputs
        modulated = (image.astype(jnp.float32) * style[:, None]).astype(jnp.bfloat16)
        energy = jnp.dot(kernel_energy, style * style, precision=lax.Precision.HIGHEST)
        demodulation = lax.rsqrt(energy + epsilon)
        convolved = jnp.zeros((COUT, length), jnp.float32)
        for tap_index, (row_step, col_step) in enumerate(tap_steps):
            product = jnp.dot(weight[tap_index], modulated, preferred_element_type=jnp.float32)
            convolved = convolved + displace(product, row_step, col_step, RES)
        output = (demodulation[:, None] * convolved).astype(jnp.bfloat16)
        grads = upstream.astype(jnp.float32)
        scaled = (grads * demodulation[:, None]).astype(jnp.bfloat16)
        norm_grad = lax.optimization_barrier(jnp.sum(grads * convolved, axis=1))
        energy_grad = -0.5 * norm_grad * demodulation ** 3
        moved = [displace(scaled, -row_step, -col_step, RES) for row_step, col_step in tap_steps]
        back_sum = jnp.zeros((CIN, length), jnp.float32)
        style_sum = jnp.zeros((CIN,), jnp.float32)
        for member in range(N_COUT):
            lower = member * group
            back_part = jnp.zeros((CIN, length), jnp.float32)
            for tap_index in range(TAPS):
                back_part = back_part + jnp.dot(weight[tap_index, lower:lower + group].T, moved[tap_index][lower:lower + group], preferred_element_type=jnp.float32)
            style_part = 2.0 * style * jnp.dot(energy_grad[lower:lower + group], kernel_energy[lower:lower + group], precision=lax.Precision.HIGHEST)
            back_sum = back_sum + round_trip(back_part)
            style_sum = style_sum + round_trip(style_part)
        input_grad = (back_sum * style[:, None]).astype(jnp.bfloat16)
        style_grad = lax.optimization_barrier(jnp.sum(back_sum * image.astype(jnp.float32), axis=1)) + style_sum
        weight_part = jnp.stack([jnp.dot(moved[tap_index], modulated.T, preferred_element_type=jnp.float32) for tap_index in range(TAPS)])
        radial = 2.0 * weight.astype(jnp.float32) * jnp.outer(energy_grad, style * style)[None]
        return (carry + weight_part + radial, (output, input_grad, style_grad))
    start = jnp.zeros((TAPS, COUT, CIN), jnp.float32)
    weight_total, (output, input_grad, style_grad) = lax.scan(step, start, (images, styles, cotangent))
    weight_grad = weight_total * (1.0 / BATCH)
    return (output, input_grad, style_grad, weight_grad)
```

```python
import functools
import math

import jax
import jax.numpy as jnp
from jax import lax
from jax.experimental import pallas as pl
from jax.experimental.pallas import tpu as pltpu
from jax.sharding import PartitionSpec as P

epsilon = 1e-08
tap_steps = [(-1, -1), (-1, 0), (-1, 1), (0, -1), (0, 0), (0, 1), (1, -1), (1, 0), (1, 1)]
TAPS = len(tap_steps)
BF16 = jnp.bfloat16
F32 = jnp.float32
HIGHEST = lax.Precision.HIGHEST
LANES = 128
ROWS = 32
VMEM = 56 * 2**20


def shifted(values, row_step, col_step, side, row, column):
    pixels = values.shape[1]
    offset = row_step * side + col_step
    if offset == 0:
        return values
    moved = pltpu.roll(values, (-offset) % pixels, 1)
    inside = None
    for step, place in ((row_step, row), (col_step, column)):
        if step:
            ok = place >= 1 if step < 0 else place < side - 1
            inside = ok if inside is None else inside & ok
    return jnp.where(inside, moved, jnp.zeros_like(moved))


def places(rows, pixels, side):
    pixel = lax.broadcasted_iota(jnp.int32, (rows, pixels), 1)
    return pixel // side, pixel % side


def back_kernel(side, n, me_ref, upstream_ref, factor_ref, weight_ref, *rest):
    out_refs, columns = rest[:n], rest[n]
    outputs, pixels = upstream_ref.shape[1:]
    block = weight_ref.shape[0] // n
    row, column = places(ROWS, pixels, side)

    @pl.loop(0, outputs // ROWS)
    def _(chunk):
        rows = pl.ds(pl.multiple_of(chunk * ROWS, ROWS), ROWS)
        scaled = (upstream_ref[0, rows, :].astype(F32) * factor_ref[0, rows, :]).astype(BF16).astype(F32)
        for tap, (row_step, col_step) in enumerate(tap_steps):
            place = pl.ds(pl.multiple_of(tap * outputs + chunk * ROWS, ROWS), ROWS)
            columns[place, :] = shifted(scaled, -row_step, -col_step, side, row, column).astype(BF16)

    for step in range(n):
        owner = lax.rem(me_ref[0] + step, n)
        rows = pl.ds(pl.multiple_of(owner * block, block), block)
        out_refs[step][0] = jnp.dot(
            weight_ref[rows, :], columns[...], preferred_element_type=F32
        ).astype(BF16)


def forward_kernel(side, n, me_ref, upstream_ref, factor_ref, squares_ref, forward_ref, weight_ref, *rest):
    maps = rest[:n]
    output_ref, energy_ref, gradient_ref, columns, scaled_ref, total = rest[n:]
    outputs, pixels = upstream_ref.shape[1:]
    block = maps[0].shape[1]
    inputs = n * block
    image = pl.program_id(0)
    row, column = places(ROWS, pixels, side)

    @pl.when(image == 0)
    def _():
        total[...] = jnp.zeros_like(total)
        energy_ref[...] = jnp.zeros_like(energy_ref)

    for step in range(n):
        owner = lax.rem(me_ref[0] + n - step, n)

        @pl.loop(0, block // ROWS)
        def _(chunk):
            rows = pl.ds(pl.multiple_of(chunk * ROWS, ROWS), ROWS)
            values = maps[step][0, rows, :].astype(F32)
            for tap, (row_step, col_step) in enumerate(tap_steps):
                place = pl.ds(pl.multiple_of(tap * inputs + owner * block + chunk * ROWS, ROWS), ROWS)
                columns[place, :] = shifted(values, row_step, col_step, side, row, column).astype(BF16)

    factor = factor_ref[0]
    upstream = upstream_ref[0].astype(F32)
    scaled_ref[...] = (upstream * factor).astype(BF16)
    convolved = jnp.dot(forward_ref[...], columns[...], preferred_element_type=F32)
    output_ref[0] = (factor * convolved).astype(BF16)
    norm_grad = jnp.sum(upstream_ref[0].astype(F32) * convolved, axis=1, keepdims=True)
    energy_grad = -0.5 * norm_grad * (factor * factor * factor)
    lane = lax.broadcasted_iota(jnp.int32, energy_ref.shape, 1)
    energy_ref[...] += jnp.where(lane == image, energy_grad, 0.0)

    for tap in range(TAPS):
        total[:, tap * outputs : (tap + 1) * outputs] += lax.dot_general(
            columns[tap * inputs : (tap + 1) * inputs, :],
            scaled_ref[...],
            (((1,), (1,)), ((), ())),
            preferred_element_type=F32,
        )

    @pl.when(image == pl.num_programs(0) - 1)
    def _():
        radial = 2.0 * lax.dot_general(
            squares_ref[...],
            energy_ref[...],
            (((1,), (1,)), ((), ())),
            precision=HIGHEST,
            preferred_element_type=F32,
        )
        for tap in range(TAPS):
            part = slice(tap * outputs, (tap + 1) * outputs)
            gradient_ref[:, part] = (
                total[:, part] + weight_ref[:, part].astype(F32) * radial
            ).astype(BF16)


def on_device(n, images, styles, weight, cotangent):
    batch, block, pixels = images.shape
    outputs = weight.shape[1]
    inputs = styles.shape[1]
    side = math.isqrt(pixels)
    me = lax.axis_index("cout")
    position = me.reshape(1).astype(jnp.int32)

    def send(values, step):
        return lax.ppermute(values, "cout", [(j, (j + step) % n) for j in range(n)])

    local_styles = lax.dynamic_slice_in_dim(styles, me * block, block, 1)
    modulated = (images.astype(F32) * local_styles[:, :, None]).astype(BF16)
    maps = [modulated] + [send(modulated, step) for step in range(1, n)]

    mine = weight.transpose(2, 0, 1).reshape(weight.shape[2], TAPS * outputs)
    by_input = lax.all_gather(mine, "dp", axis=0, tiled=True)
    cube = by_input.reshape(inputs, TAPS, outputs)
    kernel_energy = jnp.sum(jnp.square(cube.astype(F32)), axis=1)
    style_square = styles * styles
    energy = jnp.dot(style_square, kernel_energy, precision=HIGHEST)
    demodulation = lax.rsqrt(energy + epsilon)
    factor = demodulation[:, :, None]
    by_output = cube.transpose(2, 1, 0).reshape(outputs, TAPS * inputs)

    smem = pl.BlockSpec(memory_space=pltpu.SMEM)
    work = 2 * TAPS * inputs * outputs * pixels
    backs = []
    for image in range(batch):
        at = functools.partial(lambda image, i: (image, 0, 0), image)
        parts = pl.pallas_call(
            functools.partial(back_kernel, side, n),
            grid=(1,),
            out_shape=[jax.ShapeDtypeStruct((1, block, pixels), BF16)] * n,
            in_specs=[
                smem,
                pl.BlockSpec((1, outputs, pixels), at),
                pl.BlockSpec((1, outputs, 1), at),
                pl.BlockSpec(by_input.shape, lambda i: (0, 0)),
            ],
            out_specs=[pl.BlockSpec((1, block, pixels), lambda i: (0, 0, 0))] * n,
            scratch_shapes=[pltpu.VMEM((TAPS * outputs, pixels), BF16)],
            compiler_params=pltpu.CompilerParams(vmem_limit_bytes=VMEM),
            cost_estimate=pl.CostEstimate(
                flops=2 * work, bytes_accessed=8 * outputs * pixels, transcendentals=0
            ),
            name="back",
        )(position, cotangent, factor, by_input)
        backs.append([parts[0]] + [send(parts[step], step) for step in range(1, n)])

    lanes = -(-batch // LANES) * LANES
    squares = jnp.pad(style_square.T, ((0, 0), (0, lanes - batch)))
    one = lambda i: (i, 0, 0)
    whole = lambda i: (0, 0)
    output, energy_columns, gradient = pl.pallas_call(
        functools.partial(forward_kernel, side, n),
        grid=(batch,),
        out_shape=[
            jax.ShapeDtypeStruct((batch, outputs, pixels), BF16),
            jax.ShapeDtypeStruct((outputs, lanes), F32),
            jax.ShapeDtypeStruct((inputs, TAPS * outputs), BF16),
        ],
        in_specs=[
            smem,
            pl.BlockSpec((1, outputs, pixels), one),
            pl.BlockSpec((1, outputs, 1), one),
            pl.BlockSpec(squares.shape, whole),
            pl.BlockSpec(by_output.shape, whole),
            pl.BlockSpec(by_input.shape, whole),
        ]
        + [pl.BlockSpec((1, block, pixels), one)] * n,
        out_specs=[
            pl.BlockSpec((1, outputs, pixels), one),
            pl.BlockSpec((outputs, lanes), whole),
            pl.BlockSpec((inputs, TAPS * outputs), whole),
        ],
        scratch_shapes=[
            pltpu.VMEM((TAPS * inputs, pixels), BF16),
            pltpu.VMEM((outputs, pixels), BF16),
            pltpu.VMEM((inputs, TAPS * outputs), F32),
        ],
        compiler_params=pltpu.CompilerParams(vmem_limit_bytes=VMEM),
        cost_estimate=pl.CostEstimate(
            flops=3 * batch * work, bytes_accessed=16 * batch * outputs * pixels, transcendentals=0
        ),
        name="forward",
    )(position, cotangent, factor, squares, by_output, by_input, *maps)

    gradient = lax.psum_scatter(gradient, "dp", scatter_dimension=0, tiled=True)
    image_count = batch * lax.axis_size("dp")
    weight_grad = gradient.astype(F32).reshape(-1, TAPS, outputs).transpose(1, 2, 0) * (1.0 / image_count)

    energy_grad = energy_columns[:, :batch].T
    style_terms = 2.0 * styles * jnp.dot(energy_grad, kernel_energy.T, precision=HIGHEST)
    style_terms = style_terms.astype(BF16)
    style_sum = 0.0
    for step in range(n):
        part = lax.dynamic_slice_in_dim(style_terms, lax.rem(me + step, n) * block, block, 1)
        style_sum = style_sum + (send(part, step) if step else part).astype(F32)

    back_sum = 0.0
    for step in range(n):
        back_sum = back_sum + jnp.concatenate([parts[step] for parts in backs], 0).astype(F32)
    input_grad = (back_sum * local_styles[:, :, None]).astype(BF16)
    style_grad = jnp.sum(back_sum * images.astype(F32), axis=2) + style_sum
    return (output, input_grad, style_grad, weight_grad)


def solution(mesh):
    return jax.shard_map(
        functools.partial(on_device, mesh.shape["cout"]),
        mesh=mesh,
        in_specs=(
            P("dp", "cout", None),
            P("dp", None),
            P(None, "cout", "dp"),
            P("dp", "cout", None),
        ),
        out_specs=(
            P("dp", "cout", None),
            P("dp", "cout", None),
            P("dp", "cout"),
            P(None, "cout", "dp"),
        ),
        check_vma=False,
    )
```

```python
import functools
import math

import jax
import jax.numpy as jnp
from jax import lax
from jax.experimental import pallas as pl
from jax.experimental.pallas import tpu as pltpu
from jax.sharding import PartitionSpec as P

epsilon = 1e-08
tap_steps = [(-1, -1), (-1, 0), (-1, 1), (0, -1), (0, 0), (0, 1), (1, -1), (1, 0), (1, 1)]
TAPS = len(tap_steps)
BF16 = jnp.bfloat16
F32 = jnp.float32
HIGHEST = lax.Precision.HIGHEST
LANES = 128
ROWS = 32
VMEM = 56 * 2**20
MESH = pl.DeviceIdType.MESH


def shifted(values, row_step, col_step, side, row, column):
    pixels = values.shape[1]
    offset = row_step * side + col_step
    if offset == 0:
        return values
    moved = pltpu.roll(values, (-offset) % pixels, 1)
    inside = None
    for step, place in ((row_step, row), (col_step, column)):
        if step:
            ok = place >= 1 if step < 0 else place < side - 1
            inside = ok if inside is None else inside & ok
    return jnp.where(inside, moved, jnp.zeros_like(moved))


def places(rows, pixels, side):
    pixel = lax.broadcasted_iota(jnp.int32, (rows, pixels), 1)
    return pixel // side, pixel % side


def back_kernel(side, n, me_ref, upstream_ref, factor_ref, weight_ref, *rest):
    out_refs, columns, terms = rest[:n], rest[n], rest[n + 1]
    outputs, pixels = upstream_ref.shape[1:]
    block = weight_ref.shape[0] // n
    row, column = places(ROWS, pixels, side)

    @pl.loop(0, outputs // ROWS)
    def _(chunk):
        rows = pl.ds(pl.multiple_of(chunk * ROWS, ROWS), ROWS)
        scaled = (upstream_ref[0, rows, :].astype(F32) * factor_ref[0, rows, :]).astype(BF16)
        for tap, (row_step, col_step) in enumerate(tap_steps):
            place = pl.ds(pl.multiple_of(tap * outputs + chunk * ROWS, ROWS), ROWS)
            columns[place, :] = shifted(scaled, -row_step, -col_step, side, row, column).astype(BF16)

    terms[...] = jnp.dot(weight_ref[...], columns[...], preferred_element_type=F32).astype(BF16)
    for step in range(n):
        owner = lax.rem(me_ref[0] + step, n)
        out_refs[step][0] = terms[pl.ds(pl.multiple_of(owner * block, block), block), :]


def forward_kernel(side, n, me_ref, upstream_ref, factor_ref, squares_ref, weight_ref, *rest):
    maps = rest[:n]
    output_ref, energy_ref, gradient_ref, columns, scaled_ref, forward_ref, total = rest[n:]
    outputs, pixels = upstream_ref.shape[1:]
    block = maps[0].shape[1]
    inputs = n * block
    image = pl.program_id(0)
    row, column = places(ROWS, pixels, side)

    @pl.when(image == 0)
    def _():
        for tap in range(TAPS):
            forward_ref[:, tap * inputs : (tap + 1) * inputs] = weight_ref[:, tap * outputs : (tap + 1) * outputs].T
        total[...] = jnp.zeros_like(total)
        energy_ref[...] = jnp.zeros_like(energy_ref)

    for step in range(n):
        owner = lax.rem(me_ref[0] + n - step, n)

        @pl.loop(0, block // ROWS)
        def _(chunk):
            rows = pl.ds(pl.multiple_of(chunk * ROWS, ROWS), ROWS)
            values = maps[step][0, rows, :]
            for tap, (row_step, col_step) in enumerate(tap_steps):
                place = pl.ds(pl.multiple_of(tap * inputs + owner * block + chunk * ROWS, ROWS), ROWS)
                columns[place, :] = shifted(values, row_step, col_step, side, row, column).astype(BF16)

    factor = factor_ref[0]
    upstream = upstream_ref[0].astype(F32)
    scaled_ref[...] = (upstream * factor).astype(BF16)
    convolved = jnp.dot(forward_ref[...], columns[...], preferred_element_type=F32)
    output_ref[0] = (factor * convolved).astype(BF16)
    norm_grad = jnp.sum(upstream_ref[0].astype(F32) * convolved, axis=1, keepdims=True)
    energy_grad = -0.5 * norm_grad * (factor * factor * factor)
    lane = lax.broadcasted_iota(jnp.int32, energy_ref.shape, 1)
    energy_ref[...] += jnp.where(lane == image, energy_grad, 0.0)

    group = 3 * inputs
    for at in range(0, TAPS * inputs, group):
        total[at : at + group, :] += lax.dot_general(
            columns[at : at + group, :],
            scaled_ref[...],
            (((1,), (1,)), ((), ())),
            preferred_element_type=F32,
        )

    @pl.when(image == pl.num_programs(0) - 1)
    def _():
        radial = 2.0 * lax.dot_general(
            squares_ref[...],
            energy_ref[...],
            (((1,), (1,)), ((), ())),
            precision=HIGHEST,
            preferred_element_type=F32,
        )
        for tap in range(TAPS):
            part = slice(tap * outputs, (tap + 1) * outputs)
            gradient_ref[:, part] = (
                total[tap * inputs : (tap + 1) * inputs, :] + weight_ref[:, part].astype(F32) * radial
            ).astype(BF16)


def flipped(me, distances):
    place = me
    for distance in distances:
        place = place + distance * (1 - 2 * lax.rem(lax.div(me, distance), 2))
    return place


def orders(size, columns):
    distances = [1 << bit for bit in range(size.bit_length() - 1)][::-1]
    if columns % (2 * LANES) or size < 8:
        return [(slice(0, columns), distances)]
    half = columns // 2
    turned = distances[-2:-1] + distances[:-2] + distances[-1:]
    return [(slice(0, half), distances), (slice(half, columns), turned)]


def distances_of(order, slot):
    return [distance for bit, distance in enumerate(order) if (slot >> bit) & 1]


def greet(me, order):
    barrier = pltpu.get_barrier_semaphore()
    for distance in order:
        pl.semaphore_signal(barrier, inc=1, device_id={"dp": flipped(me, [distance])}, device_id_type=MESH)
    pl.semaphore_wait(barrier, len(order))


def gather_kernel(size, parts, taps, mine_ref, after_ref, whole_ref, energy_ref, send_sem, recv_sem, *held):
    me = lax.axis_index("dp")
    del after_ref
    steps = len(parts[0][1])
    for part, (columns, _) in enumerate(parts):
        held[part][0] = mine_ref[:, columns]
    greet(me, parts[0][1])
    copies = [None] * len(parts)
    for step in range(steps):
        for part, (_, order) in enumerate(parts):
            if step:
                copies[part].wait()
            count = 1 << step
            copies[part] = pltpu.make_async_remote_copy(
                src_ref=held[part].at[0:count],
                dst_ref=held[part].at[count : 2 * count],
                send_sem=send_sem.at[part, step],
                recv_sem=recv_sem.at[part, step],
                device_id={"dp": flipped(me, [order[step]])},
                device_id_type=MESH,
            )
            copies[part].start()
    for copy in copies:
        copy.wait()
    outputs = energy_ref.shape[2]
    for part, (columns, order) in enumerate(parts):
        for slot in range(size):
            owner = flipped(me, distances_of(order, slot))
            whole_ref[owner, :, columns] = held[part][slot]
    for slot in range(size):
        energy = None
        for tap in range(taps):
            value = whole_ref[slot, :, tap * outputs : (tap + 1) * outputs].astype(F32)
            energy = value * value if energy is None else energy + value * value
        energy_ref[slot] = energy


def reduce_kernel(size, parts, terms_ref, total_ref, send_sem, recv_sem, *scratch):
    me = lax.axis_index("dp")
    steps = len(parts[0][1])
    work, came = scratch[: len(parts)], scratch[len(parts) :]
    greet(me, parts[0][1])
    copies = [None] * len(parts)
    for step in range(steps - 1, -1, -1):
        count = 1 << step
        for part, (columns, order) in enumerate(parts):
            if step == steps - 1:
                for slot in range(size):
                    owner = flipped(me, distances_of(order, slot))
                    work[part][slot] = terms_ref[owner, :, columns]
            else:
                copies[part].wait()
                for slot in range(2 * count):
                    work[part][slot] = (
                        work[part][slot].astype(F32) + came[part][2 * count + slot].astype(F32)
                    ).astype(BF16)
            copies[part] = pltpu.make_async_remote_copy(
                src_ref=work[part].at[count : 2 * count],
                dst_ref=came[part].at[count : 2 * count],
                send_sem=send_sem.at[part, step],
                recv_sem=recv_sem.at[part, step],
                device_id={"dp": flipped(me, [order[step]])},
                device_id_type=MESH,
            )
            copies[part].start()
    for part, (columns, _) in enumerate(parts):
        copies[part].wait()
        total_ref[:, columns] = work[part][0].astype(F32) + came[part][1].astype(F32)


def modulate_kernel(images_ref, styles_ref, modulated_ref):
    modulated_ref[...] = (images_ref[...].astype(F32) * styles_ref[...]).astype(BF16)


def finish_kernel(n, after_ref, images_ref, styles_ref, *rest):
    del after_ref
    parts, (input_ref, style_ref) = rest[:-2], rest[-2:]
    for image in range(images_ref.shape[0]):
        total = 0.0
        for part in parts[image * n : (image + 1) * n]:
            total = total + part[0].astype(F32)
        input_ref[image] = (total * styles_ref[image]).astype(BF16)
        style_ref[image] = jnp.sum(total * images_ref[image].astype(F32), axis=1, keepdims=True)


def exchange_scratch(size, parts, rows, buffers):
    steps = len(parts[0][1])
    return [pltpu.SemaphoreType.DMA((len(parts), steps))] * 2 + [
        pltpu.VMEM((size, rows, columns.stop - columns.start), BF16) for columns, _ in parts
    ] * buffers


def gather_rows(mine, after, size):
    rows, columns = mine.shape
    parts = orders(size, columns)
    vmem = pl.BlockSpec(memory_space=pltpu.VMEM)
    return pl.pallas_call(
        functools.partial(gather_kernel, size, parts, TAPS),
        out_shape=[
            jax.ShapeDtypeStruct((size, rows, columns), BF16),
            jax.ShapeDtypeStruct((size, rows, columns // TAPS), F32),
        ],
        in_specs=[vmem, pl.BlockSpec(memory_space=pl.ANY)],
        out_specs=[vmem, vmem],
        scratch_shapes=exchange_scratch(size, parts, rows, 1),
        compiler_params=pltpu.CompilerParams(collective_id=0, has_side_effects=True, vmem_limit_bytes=VMEM),
        name="gather",
    )(mine, after)


def reduce_rows(terms, size):
    _, rows, columns = terms.shape
    parts = orders(size, columns)
    vmem = pl.BlockSpec(memory_space=pltpu.VMEM)
    return pl.pallas_call(
        functools.partial(reduce_kernel, size, parts),
        out_shape=jax.ShapeDtypeStruct((rows, columns), F32),
        in_specs=[vmem],
        out_specs=vmem,
        scratch_shapes=exchange_scratch(size, parts, rows, 2),
        compiler_params=pltpu.CompilerParams(collective_id=1, has_side_effects=True, vmem_limit_bytes=VMEM),
        name="reduce",
    )(terms)


def on_device(n, images, styles, weight, cotangent):
    batch, block, pixels = images.shape
    outputs = weight.shape[1]
    inputs = styles.shape[1]
    side = math.isqrt(pixels)
    me = lax.axis_index("cout")
    position = me.reshape(1).astype(jnp.int32)

    def send(values, step):
        return lax.ppermute(values, "cout", [(j, (j + step) % n) for j in range(n)])

    local_styles = lax.dynamic_slice_in_dim(styles, me * block, block, 1)
    vmem = pl.BlockSpec(memory_space=pltpu.VMEM)
    plan = pltpu.CompilerParams(vmem_limit_bytes=VMEM)
    one_image = pl.BlockSpec((1, block, pixels), lambda i: (i, 0, 0))
    modulated = pl.pallas_call(
        modulate_kernel,
        grid=(batch,),
        out_shape=jax.ShapeDtypeStruct(images.shape, BF16),
        in_specs=[one_image, pl.BlockSpec((1, block, 1), lambda i: (i, 0, 0))],
        out_specs=one_image,
        compiler_params=plan,
        name="modulate",
    )(images, local_styles[:, :, None])
    maps = [modulated] + [send(modulated, step) for step in range(1, n)]

    mine = weight.transpose(2, 0, 1).reshape(weight.shape[2], TAPS * outputs)
    size = lax.axis_size("dp")
    by_input, kernel_energy = gather_rows(mine, modulated, size)
    by_input = by_input.reshape(inputs, TAPS * outputs)
    kernel_energy = kernel_energy.reshape(inputs, outputs)
    style_square = styles * styles
    energy = jnp.dot(style_square, kernel_energy, precision=HIGHEST)
    demodulation = lax.rsqrt(energy + epsilon)
    factor = demodulation[:, :, None]

    smem = pl.BlockSpec(memory_space=pltpu.SMEM)
    work = 2 * TAPS * inputs * outputs * pixels
    backs = []
    for image in range(batch):
        at = functools.partial(lambda image, i: (image, 0, 0), image)
        parts = pl.pallas_call(
            functools.partial(back_kernel, side, n),
            grid=(1,),
            out_shape=[jax.ShapeDtypeStruct((1, block, pixels), BF16)] * n,
            in_specs=[
                smem,
                pl.BlockSpec((1, outputs, pixels), at),
                pl.BlockSpec((1, outputs, 1), at),
                pl.BlockSpec(by_input.shape, lambda i: (0, 0)),
            ],
            out_specs=[pl.BlockSpec((1, block, pixels), lambda i: (0, 0, 0))] * n,
            scratch_shapes=[pltpu.VMEM((TAPS * outputs, pixels), BF16), pltpu.VMEM((inputs, pixels), BF16)],
            compiler_params=pltpu.CompilerParams(vmem_limit_bytes=VMEM),
            cost_estimate=pl.CostEstimate(flops=work, bytes_accessed=8 * outputs * pixels, transcendentals=0),
            name="back",
        )(position, cotangent, factor, by_input)
        backs.append([parts[0]] + [send(parts[step], step) for step in range(1, n)])

    lanes = -(-batch // LANES) * LANES
    squares = jnp.pad(style_square.T, ((0, 0), (0, lanes - batch)))
    one = lambda i: (i, 0, 0)
    whole = lambda i: (0, 0)
    output, energy_columns, gradient = pl.pallas_call(
        functools.partial(forward_kernel, side, n),
        grid=(batch,),
        out_shape=[
            jax.ShapeDtypeStruct((batch, outputs, pixels), BF16),
            jax.ShapeDtypeStruct((outputs, lanes), F32),
            jax.ShapeDtypeStruct((inputs, TAPS * outputs), BF16),
        ],
        in_specs=[
            smem,
            pl.BlockSpec((1, outputs, pixels), one),
            pl.BlockSpec((1, outputs, 1), one),
            pl.BlockSpec(squares.shape, whole),
            pl.BlockSpec(by_input.shape, whole),
        ]
        + [pl.BlockSpec((1, block, pixels), one)] * n,
        out_specs=[
            pl.BlockSpec((1, outputs, pixels), one),
            pl.BlockSpec((outputs, lanes), whole),
            pl.BlockSpec((inputs, TAPS * outputs), whole),
        ],
        scratch_shapes=[
            pltpu.VMEM((TAPS * inputs, pixels), BF16),
            pltpu.VMEM((outputs, pixels), BF16),
            pltpu.VMEM((outputs, TAPS * inputs), BF16),
            pltpu.VMEM((TAPS * inputs, outputs), F32),
        ],
        compiler_params=pltpu.CompilerParams(vmem_limit_bytes=VMEM),
        cost_estimate=pl.CostEstimate(
            flops=2 * batch * work, bytes_accessed=16 * batch * outputs * pixels, transcendentals=0
        ),
        name="forward",
    )(position, cotangent, factor, squares, by_input, *maps)

    gradient = reduce_rows(gradient.reshape(size, inputs // size, TAPS * outputs), size)
    image_count = batch * lax.axis_size("dp")
    weight_grad = gradient.reshape(-1, TAPS, outputs).transpose(1, 2, 0) * (1.0 / image_count)

    energy_grad = energy_columns[:, :batch].T
    style_terms = 2.0 * styles * jnp.dot(energy_grad, kernel_energy.T, precision=HIGHEST)
    style_terms = style_terms.astype(BF16)
    style_sum = 0.0
    for step in range(n):
        part = lax.dynamic_slice_in_dim(style_terms, lax.rem(me + step, n) * block, block, 1)
        style_sum = style_sum + (send(part, step) if step else part).astype(F32)

    input_grad, style_part = pl.pallas_call(
        functools.partial(finish_kernel, n),
        out_shape=[
            jax.ShapeDtypeStruct(images.shape, BF16),
            jax.ShapeDtypeStruct((batch, block, 1), F32),
        ],
        in_specs=[pl.BlockSpec(memory_space=pl.ANY)] + [vmem] * (2 + n * batch),
        out_specs=[vmem, vmem],
        compiler_params=plan,
        name="finish",
    )(gradient, images, local_styles[:, :, None], *[part for parts in backs for part in parts])
    style_grad = style_part[:, :, 0] + style_sum
    return (output, input_grad, style_grad, weight_grad)


def solution(mesh):
    return jax.shard_map(
        functools.partial(on_device, mesh.shape["cout"]),
        mesh=mesh,
        in_specs=(
            P("dp", "cout", None),
            P("dp", None),
            P(None, "cout", "dp"),
            P("dp", "cout", None),
        ),
        out_specs=(
            P("dp", "cout", None),
            P("dp", "cout", None),
            P("dp", "cout"),
            P(None, "cout", "dp"),
        ),
        check_vma=False,
    )
```

```python
import functools
import math

import jax
import jax.numpy as jnp
from jax import lax
from jax.experimental import pallas as pl
from jax.experimental.pallas import tpu as pltpu
from jax.sharding import PartitionSpec as P

epsilon = 1e-08
TAPS = 9
BF16 = jnp.bfloat16
F32 = jnp.float32
HIGHEST = lax.Precision.HIGHEST
LANES = 128
VMEM = 56 * 2**20
MESH = pl.DeviceIdType.MESH


def spread(columns, at, lane, stride, values, side):
    rows, width = values.shape
    column = lax.broadcasted_iota(jnp.int32, values.shape, 0) % side
    for group, moved in enumerate(
        (
            jnp.where(column >= 1, pltpu.roll(values, 1, 0), 0.0),
            values,
            jnp.where(column < side - 1, pltpu.roll(values, rows - 1, 0), 0.0),
        )
    ):
        start = group * stride + lane
        columns[side + at : side + at + rows, start : start + width] = moved.astype(BF16)


def clear_margins(columns, side):
    margin = jnp.zeros((side, columns.shape[1]), BF16)
    columns[:side, :] = margin
    columns[columns.shape[0] - side :, :] = margin


def convolve(columns, weights, pixels, side):
    depth = columns.shape[1]
    total = 0.0
    for row in range(3):
        total = total + jnp.dot(
            columns[row * side : row * side + pixels, :],
            weights[row * depth : (row + 1) * depth, :],
            preferred_element_type=F32,
        )
    return total


def back_kernel(side, n, me_ref, upstream_ref, factor_ref, weight_ref, *rest):
    out_refs, columns, turned, terms = rest[:n], rest[n], rest[n + 1], rest[n + 2]
    outputs, pixels = upstream_ref.shape[1:]
    block = weight_ref.shape[0] // n

    @pl.when(pl.program_id(0) == 0)
    def _():
        clear_margins(columns, side)
        for tap in range(TAPS):
            mirror = TAPS - 1 - tap
            turned[mirror * outputs : (mirror + 1) * outputs, :] = weight_ref[
                :, tap * outputs : (tap + 1) * outputs
            ].T

    for at in range(0, pixels, LANES):
        scaled = upstream_ref[0, :, at : at + LANES].astype(F32) * factor_ref[0]
        spread(columns, at, 0, outputs, scaled.T, side)
    terms[...] = convolve(columns, turned, pixels, side).astype(BF16).T
    for step in range(n):
        owner = lax.rem(me_ref[0] + step, n)
        out_refs[step][0] = terms[pl.ds(pl.multiple_of(owner * block, block), block), :]


def forward_kernel(side, n, me_ref, upstream_ref, factor_ref, squares_ref, weight_ref, *rest):
    maps = rest[:n]
    output_ref, energy_ref, gradient_ref, columns, forward_ref, radial_ref, total = rest[n:]
    outputs, pixels = upstream_ref.shape[1:]
    block = maps[0].shape[2]
    inputs = n * block
    image = pl.program_id(0)

    def rows_of(step):
        owner = lax.rem(me_ref[0] + n - step, n)
        return pl.ds(pl.multiple_of(owner * block, block), block)

    @pl.when(image == 0)
    def _():
        clear_margins(columns, side)
        for tap in range(TAPS):
            for step in range(n):
                at = tap * inputs + step * block
                forward_ref[at : at + block, :] = weight_ref[rows_of(step), tap * outputs : (tap + 1) * outputs]
        total[...] = jnp.zeros_like(total)
        energy_ref[...] = jnp.zeros_like(energy_ref)

    for step in range(n):
        for at in range(0, pixels, LANES):
            spread(columns, at, step * block, inputs, maps[step][0, at : at + LANES, :].astype(F32), side)

    factor = factor_ref[0]
    convolved = convolve(columns, forward_ref, pixels, side).T
    output_ref[0] = (factor * convolved).astype(BF16)
    upstream = upstream_ref[0].astype(F32)
    norm_grad = jnp.sum(upstream * convolved, axis=1, keepdims=True)
    energy_grad = -0.5 * norm_grad * (factor * factor * factor)
    lane = lax.broadcasted_iota(jnp.int32, energy_ref.shape, 1)
    energy_ref[...] += jnp.where(lane == image, energy_grad, 0.0)

    scaled = (upstream * factor).astype(BF16)
    depth = 3 * inputs
    for row in range(3):
        total[:, row * depth : (row + 1) * depth] += jnp.dot(
            scaled, columns[row * side : row * side + pixels, :], preferred_element_type=F32
        )

    @pl.when(image == pl.num_programs(0) - 1)
    def _():
        radial_ref[...] = 2.0 * lax.dot_general(
            squares_ref[...],
            energy_ref[...],
            (((1,), (1,)), ((), ())),
            precision=HIGHEST,
            preferred_element_type=F32,
        )
        for tap in range(TAPS):
            part = slice(tap * outputs, (tap + 1) * outputs)
            for step in range(n):
                at = tap * inputs + step * block
                gradient_ref[rows_of(step), part] = (
                    total[:, at : at + block].T
                    + weight_ref[rows_of(step), part].astype(F32) * radial_ref[rows_of(step), :]
                ).astype(BF16)


def flipped(me, distances):
    place = me
    for distance in distances:
        place = place + distance * (1 - 2 * lax.rem(lax.div(me, distance), 2))
    return place


def orders(size, columns):
    distances = [1 << bit for bit in range(size.bit_length() - 1)][::-1]
    if columns % (2 * LANES) or size < 8:
        return [(slice(0, columns), distances)]
    half = columns // 2
    turned = distances[-2:-1] + distances[:-2] + distances[-1:]
    return [(slice(0, half), distances), (slice(half, columns), turned)]


def distances_of(order, slot):
    return [distance for bit, distance in enumerate(order) if (slot >> bit) & 1]


def greet(me, order):
    barrier = pltpu.get_barrier_semaphore()
    for distance in order:
        pl.semaphore_signal(barrier, inc=1, device_id={"dp": flipped(me, [distance])}, device_id_type=MESH)
    pl.semaphore_wait(barrier, len(order))


def gather_kernel(size, parts, taps, mine_ref, after_ref, whole_ref, energy_ref, send_sem, recv_sem, *held):
    me = lax.axis_index("dp")
    del after_ref
    steps = len(parts[0][1])
    for part, (columns, _) in enumerate(parts):
        held[part][0] = mine_ref[:, columns]
    greet(me, parts[0][1])
    copies = [None] * len(parts)
    for step in range(steps):
        for part, (_, order) in enumerate(parts):
            if step:
                copies[part].wait()
            count = 1 << step
            copies[part] = pltpu.make_async_remote_copy(
                src_ref=held[part].at[0:count],
                dst_ref=held[part].at[count : 2 * count],
                send_sem=send_sem.at[part, step],
                recv_sem=recv_sem.at[part, step],
                device_id={"dp": flipped(me, [order[step]])},
                device_id_type=MESH,
            )
            copies[part].start()
    for copy in copies:
        copy.wait()
    outputs = energy_ref.shape[2]
    for part, (columns, order) in enumerate(parts):
        for slot in range(size):
            owner = flipped(me, distances_of(order, slot))
            whole_ref[owner, :, columns] = held[part][slot]
    for slot in range(size):
        energy = None
        for tap in range(taps):
            value = whole_ref[slot, :, tap * outputs : (tap + 1) * outputs].astype(F32)
            energy = value * value if energy is None else energy + value * value
        energy_ref[slot] = energy


def reduce_kernel(size, parts, terms_ref, total_ref, send_sem, recv_sem, *scratch):
    me = lax.axis_index("dp")
    steps = len(parts[0][1])
    work, came = scratch[: len(parts)], scratch[len(parts) :]
    greet(me, parts[0][1])
    copies = [None] * len(parts)
    for step in range(steps - 1, -1, -1):
        count = 1 << step
        for part, (columns, order) in enumerate(parts):
            if step == steps - 1:
                for slot in range(size):
                    owner = flipped(me, distances_of(order, slot))
                    work[part][slot] = terms_ref[owner, :, columns]
            else:
                copies[part].wait()
                for slot in range(2 * count):
                    work[part][slot] = (
                        work[part][slot].astype(F32) + came[part][2 * count + slot].astype(F32)
                    ).astype(BF16)
            copies[part] = pltpu.make_async_remote_copy(
                src_ref=work[part].at[count : 2 * count],
                dst_ref=came[part].at[count : 2 * count],
                send_sem=send_sem.at[part, step],
                recv_sem=recv_sem.at[part, step],
                device_id={"dp": flipped(me, [order[step]])},
                device_id_type=MESH,
            )
            copies[part].start()
    for part, (columns, _) in enumerate(parts):
        copies[part].wait()
        total_ref[:, columns] = work[part][0].astype(F32) + came[part][1].astype(F32)


def modulate_kernel(images_ref, styles_ref, modulated_ref):
    modulated_ref[0] = (images_ref[0].astype(F32) * styles_ref[0]).astype(BF16).T


def finish_kernel(after_ref, images_ref, styles_ref, *rest):
    del after_ref
    parts, (input_ref, style_ref) = rest[:-2], rest[-2:]
    total = 0.0
    for part in parts:
        total = total + part[0].astype(F32)
    input_ref[0] = (total * styles_ref[0]).astype(BF16)
    style_ref[0] = jnp.sum(total * images_ref[0].astype(F32), axis=1, keepdims=True)


def exchange_scratch(size, parts, rows, buffers):
    steps = len(parts[0][1])
    return [pltpu.SemaphoreType.DMA((len(parts), steps))] * 2 + [
        pltpu.VMEM((size, rows, columns.stop - columns.start), BF16) for columns, _ in parts
    ] * buffers


def gather_rows(mine, after, size):
    rows, columns = mine.shape
    parts = orders(size, columns)
    vmem = pl.BlockSpec(memory_space=pltpu.VMEM)
    return pl.pallas_call(
        functools.partial(gather_kernel, size, parts, TAPS),
        out_shape=[
            jax.ShapeDtypeStruct((size, rows, columns), BF16),
            jax.ShapeDtypeStruct((size, rows, columns // TAPS), F32),
        ],
        in_specs=[vmem, pl.BlockSpec(memory_space=pl.ANY)],
        out_specs=[vmem, vmem],
        scratch_shapes=exchange_scratch(size, parts, rows, 1),
        compiler_params=pltpu.CompilerParams(collective_id=0, has_side_effects=True, vmem_limit_bytes=VMEM),
        name="gather",
    )(mine, after)


def reduce_rows(terms, size):
    _, rows, columns = terms.shape
    parts = orders(size, columns)
    vmem = pl.BlockSpec(memory_space=pltpu.VMEM)
    return pl.pallas_call(
        functools.partial(reduce_kernel, size, parts),
        out_shape=jax.ShapeDtypeStruct((rows, columns), F32),
        in_specs=[vmem],
        out_specs=vmem,
        scratch_shapes=exchange_scratch(size, parts, rows, 2),
        compiler_params=pltpu.CompilerParams(collective_id=1, has_side_effects=True, vmem_limit_bytes=VMEM),
        name="reduce",
    )(terms)


def on_device(n, images, styles, weight, cotangent):
    batch, block, pixels = images.shape
    outputs = weight.shape[1]
    inputs = styles.shape[1]
    side = math.isqrt(pixels)
    me = lax.axis_index("cout")
    position = me.reshape(1).astype(jnp.int32)

    def send(values, step):
        return lax.ppermute(values, "cout", [(j, (j + step) % n) for j in range(n)])

    local_styles = lax.dynamic_slice_in_dim(styles, me * block, block, 1)
    vmem = pl.BlockSpec(memory_space=pltpu.VMEM)
    plan = pltpu.CompilerParams(vmem_limit_bytes=VMEM)
    one_image = pl.BlockSpec((1, block, pixels), lambda i: (i, 0, 0))
    modulated = pl.pallas_call(
        modulate_kernel,
        grid=(batch,),
        out_shape=jax.ShapeDtypeStruct((batch, pixels, block), BF16),
        in_specs=[one_image, pl.BlockSpec((1, block, 1), lambda i: (i, 0, 0))],
        out_specs=pl.BlockSpec((1, pixels, block), lambda i: (i, 0, 0)),
        compiler_params=plan,
        name="modulate",
    )(images, local_styles[:, :, None])
    maps = [modulated] + [send(modulated, step) for step in range(1, n)]

    mine = weight.transpose(2, 0, 1).reshape(weight.shape[2], TAPS * outputs)
    size = lax.axis_size("dp")
    by_input, kernel_energy = gather_rows(mine, modulated, size)
    by_input = by_input.reshape(inputs, TAPS * outputs)
    kernel_energy = kernel_energy.reshape(inputs, outputs)
    style_square = styles * styles
    energy = jnp.dot(style_square, kernel_energy, precision=HIGHEST)
    demodulation = lax.rsqrt(energy + epsilon)
    factor = demodulation[:, :, None]

    smem = pl.BlockSpec(memory_space=pltpu.SMEM)
    work = 2 * TAPS * inputs * outputs * pixels
    one = lambda i: (i, 0, 0)
    whole = lambda i: (0, 0)
    parts = pl.pallas_call(
        functools.partial(back_kernel, side, n),
        grid=(batch,),
        out_shape=[jax.ShapeDtypeStruct((batch, block, pixels), BF16)] * n,
        in_specs=[
            smem,
            pl.BlockSpec((1, outputs, pixels), one),
            pl.BlockSpec((1, outputs, 1), one),
            pl.BlockSpec(by_input.shape, whole),
        ],
        out_specs=[pl.BlockSpec((1, block, pixels), one)] * n,
        scratch_shapes=[
            pltpu.VMEM((pixels + 2 * side, 3 * outputs), BF16),
            pltpu.VMEM((TAPS * outputs, inputs), BF16),
            pltpu.VMEM((inputs, pixels), BF16),
        ],
        compiler_params=plan,
        cost_estimate=pl.CostEstimate(
            flops=batch * work, bytes_accessed=8 * batch * outputs * pixels, transcendentals=0
        ),
        name="back",
    )(position, cotangent, factor, by_input)
    backs = [send(part, step) if step else part for step, part in enumerate(parts)]

    lanes = -(-batch // LANES) * LANES
    squares = jnp.pad(style_square.T, ((0, 0), (0, lanes - batch)))
    output, energy_columns, gradient = pl.pallas_call(
        functools.partial(forward_kernel, side, n),
        grid=(batch,),
        out_shape=[
            jax.ShapeDtypeStruct((batch, outputs, pixels), BF16),
            jax.ShapeDtypeStruct((outputs, lanes), F32),
            jax.ShapeDtypeStruct((inputs, TAPS * outputs), BF16),
        ],
        in_specs=[
            smem,
            pl.BlockSpec((1, outputs, pixels), one),
            pl.BlockSpec((1, outputs, 1), one),
            pl.BlockSpec(squares.shape, whole),
            pl.BlockSpec(by_input.shape, whole),
        ]
        + [pl.BlockSpec((1, pixels, block), one)] * n,
        out_specs=[
            pl.BlockSpec((1, outputs, pixels), one),
            pl.BlockSpec((outputs, lanes), whole),
            pl.BlockSpec((inputs, TAPS * outputs), whole),
        ],
        scratch_shapes=[
            pltpu.VMEM((pixels + 2 * side, 3 * inputs), BF16),
            pltpu.VMEM((TAPS * inputs, outputs), BF16),
            pltpu.VMEM((inputs, outputs), F32),
            pltpu.VMEM((outputs, TAPS * inputs), F32),
        ],
        compiler_params=pltpu.CompilerParams(vmem_limit_bytes=VMEM),
        cost_estimate=pl.CostEstimate(
            flops=2 * batch * work, bytes_accessed=16 * batch * outputs * pixels, transcendentals=0
        ),
        name="forward",
    )(position, cotangent, factor, squares, by_input, *maps)

    gradient = reduce_rows(gradient.reshape(size, inputs // size, TAPS * outputs), size)
    image_count = batch * lax.axis_size("dp")
    weight_grad = gradient.reshape(-1, TAPS, outputs).transpose(1, 2, 0) * (1.0 / image_count)

    energy_grad = energy_columns[:, :batch].T
    style_terms = 2.0 * styles * jnp.dot(energy_grad, kernel_energy.T, precision=HIGHEST)
    style_terms = style_terms.astype(BF16)
    style_sum = 0.0
    for step in range(n):
        part = lax.dynamic_slice_in_dim(style_terms, lax.rem(me + step, n) * block, block, 1)
        style_sum = style_sum + (send(part, step) if step else part).astype(F32)

    input_grad, style_part = pl.pallas_call(
        finish_kernel,
        grid=(batch,),
        out_shape=[
            jax.ShapeDtypeStruct(images.shape, BF16),
            jax.ShapeDtypeStruct((batch, block, 1), F32),
        ],
        in_specs=[pl.BlockSpec(memory_space=pl.ANY), one_image, pl.BlockSpec((1, block, 1), one)]
        + [one_image] * n,
        out_specs=[one_image, pl.BlockSpec((1, block, 1), one)],
        compiler_params=plan,
        name="finish",
    )(gradient, images, local_styles[:, :, None], *backs)
    style_grad = style_part[:, :, 0] + style_sum
    return (output, input_grad, style_grad, weight_grad)


def solution(mesh):
    return jax.shard_map(
        functools.partial(on_device, mesh.shape["cout"]),
        mesh=mesh,
        in_specs=(
            P("dp", "cout", None),
            P("dp", None),
            P(None, "cout", "dp"),
            P("dp", "cout", None),
        ),
        out_specs=(
            P("dp", "cout", None),
            P("dp", "cout", None),
            P("dp", "cout"),
            P(None, "cout", "dp"),
        ),
        check_vma=False,
    )
```

```python
import functools
import math

import jax
import jax.numpy as jnp
from jax import lax
from jax.experimental import pallas as pl
from jax.experimental.pallas import tpu as pltpu
from jax.sharding import PartitionSpec as P

epsilon = 1e-08
TAPS = 9
BF16 = jnp.bfloat16
F32 = jnp.float32
HIGHEST = lax.Precision.HIGHEST
LANES = 128
VMEM = 56 * 2**20
MESH = pl.DeviceIdType.MESH


def spread(columns, at, lane, stride, values, side):
    rows, width = values.shape
    column = lax.broadcasted_iota(jnp.int32, values.shape, 0) % side
    for group, moved in enumerate(
        (
            jnp.where(column >= 1, pltpu.roll(values, 1, 0), 0.0),
            values,
            jnp.where(column < side - 1, pltpu.roll(values, rows - 1, 0), 0.0),
        )
    ):
        start = group * stride + lane
        columns[side + at : side + at + rows, start : start + width] = moved.astype(BF16)


def clear_margins(columns, side):
    margin = jnp.zeros((side, columns.shape[1]), BF16)
    columns[:side, :] = margin
    columns[columns.shape[0] - side :, :] = margin


def convolve(columns, weights, pixels, side):
    depth = columns.shape[1]
    total = 0.0
    for row in range(3):
        total = total + jnp.dot(
            columns[row * side : row * side + pixels, :],
            weights[row * depth : (row + 1) * depth, :],
            preferred_element_type=F32,
        )
    return total


def back_kernel(side, n, me_ref, upstream_ref, factor_ref, weight_ref, *rest):
    out_refs, columns, turned, terms = rest[:n], rest[n], rest[n + 1], rest[n + 2]
    outputs, pixels = upstream_ref.shape[1:]
    block = weight_ref.shape[0] // n

    @pl.when(pl.program_id(0) == 0)
    def _():
        clear_margins(columns, side)
        for tap in range(TAPS):
            mirror = TAPS - 1 - tap
            turned[mirror * outputs : (mirror + 1) * outputs, :] = weight_ref[
                :, tap * outputs : (tap + 1) * outputs
            ].T

    for at in range(0, pixels, LANES):
        scaled = upstream_ref[0, :, at : at + LANES].astype(F32) * factor_ref[0]
        spread(columns, at, 0, outputs, scaled.T, side)
    terms[...] = convolve(columns, turned, pixels, side).astype(BF16).T
    for step in range(n):
        owner = lax.rem(me_ref[0] + step, n)
        out_refs[step][0] = terms[pl.ds(pl.multiple_of(owner * block, block), block), :]


def forward_kernel(side, n, me_ref, upstream_ref, factor_ref, squares_ref, weight_ref, *rest):
    maps = rest[:n]
    output_ref, energy_ref, gradient_ref, columns, forward_ref, radial_ref, total = rest[n:]
    outputs, pixels = upstream_ref.shape[1:]
    block = maps[0].shape[2]
    inputs = n * block
    image = pl.program_id(0)

    def rows_of(step):
        owner = lax.rem(me_ref[0] + n - step, n)
        return pl.ds(pl.multiple_of(owner * block, block), block)

    @pl.when(image == 0)
    def _():
        clear_margins(columns, side)
        for tap in range(TAPS):
            for step in range(n):
                at = tap * inputs + step * block
                forward_ref[at : at + block, :] = weight_ref[rows_of(step), tap * outputs : (tap + 1) * outputs]
        total[...] = jnp.zeros_like(total)
        energy_ref[...] = jnp.zeros_like(energy_ref)

    for step in range(n):
        for at in range(0, pixels, LANES):
            spread(columns, at, step * block, inputs, maps[step][0, at : at + LANES, :].astype(F32), side)

    factor = factor_ref[0]
    convolved = convolve(columns, forward_ref, pixels, side).T
    output_ref[0] = (factor * convolved).astype(BF16)
    upstream = upstream_ref[0].astype(F32)
    norm_grad = jnp.sum(upstream * convolved, axis=1, keepdims=True)
    energy_grad = -0.5 * norm_grad * (factor * factor * factor)
    lane = lax.broadcasted_iota(jnp.int32, energy_ref.shape, 1)
    energy_ref[...] += jnp.where(lane == image, energy_grad, 0.0)

    scaled = (upstream * factor).astype(BF16)
    depth = 3 * inputs
    for row in range(3):
        total[:, row * depth : (row + 1) * depth] += jnp.dot(
            scaled, columns[row * side : row * side + pixels, :], preferred_element_type=F32
        )

    @pl.when(image == pl.num_programs(0) - 1)
    def _():
        radial_ref[...] = 2.0 * lax.dot_general(
            squares_ref[...],
            energy_ref[...],
            (((1,), (1,)), ((), ())),
            precision=HIGHEST,
            preferred_element_type=F32,
        )
        for tap in range(TAPS):
            part = slice(tap * outputs, (tap + 1) * outputs)
            for step in range(n):
                at = tap * inputs + step * block
                gradient_ref[rows_of(step), part] = (
                    total[:, at : at + block].T
                    + weight_ref[rows_of(step), part].astype(F32) * radial_ref[rows_of(step), :]
                ).astype(BF16)


def flipped(me, distances):
    place = me
    for distance in distances:
        place = place + distance * (1 - 2 * lax.rem(lax.div(me, distance), 2))
    return place


def orders(size, columns):
    distances = [1 << bit for bit in range(size.bit_length() - 1)][::-1]
    if columns % (3 * LANES) or size < 8:
        return [(slice(0, columns), distances)]
    third = columns // 3
    turned = distances[-2:-1] + distances[:-2] + distances[-1:]
    return [(slice(part * third, (part + 1) * third), (distances, turned, distances)[part]) for part in range(3)]


def distances_of(order, slot):
    return [distance for bit, distance in enumerate(order) if (slot >> bit) & 1]


def greet(me, order):
    barrier = pltpu.get_barrier_semaphore()
    for distance in order:
        pl.semaphore_signal(barrier, inc=1, device_id={"dp": flipped(me, [distance])}, device_id_type=MESH)
    pl.semaphore_wait(barrier, len(order))


def gather_kernel(size, parts, taps, mine_ref, after_ref, whole_ref, energy_ref, send_sem, recv_sem, *held):
    me = lax.axis_index("dp")
    del after_ref
    steps = len(parts[0][1])
    for part, (columns, _) in enumerate(parts):
        held[part][0] = mine_ref[:, columns]
    greet(me, parts[0][1])
    copies = [None] * len(parts)
    for step in range(steps):
        for part, (_, order) in enumerate(parts):
            if step:
                copies[part].wait()
            count = 1 << step
            copies[part] = pltpu.make_async_remote_copy(
                src_ref=held[part].at[0:count],
                dst_ref=held[part].at[count : 2 * count],
                send_sem=send_sem.at[part, step],
                recv_sem=recv_sem.at[part, step],
                device_id={"dp": flipped(me, [order[step]])},
                device_id_type=MESH,
            )
            copies[part].start()
    for copy in copies:
        copy.wait()
    outputs = energy_ref.shape[2]
    for part, (columns, order) in enumerate(parts):
        for slot in range(size):
            owner = flipped(me, distances_of(order, slot))
            whole_ref[owner, :, columns] = held[part][slot]
    for slot in range(size):
        energy = None
        for tap in range(taps):
            value = whole_ref[slot, :, tap * outputs : (tap + 1) * outputs].astype(F32)
            energy = value * value if energy is None else energy + value * value
        energy_ref[slot] = energy


def reduce_kernel(size, parts, scale, terms_ref, total_ref, send_sem, recv_sem, *scratch):
    me = lax.axis_index("dp")
    steps = len(parts[0][1])
    work, came = scratch[: len(parts)], scratch[len(parts) :]
    greet(me, parts[0][1])
    copies = [None] * len(parts)
    for step in range(steps - 1, -1, -1):
        count = 1 << step
        for part, (columns, order) in enumerate(parts):
            if step == steps - 1:
                for slot in range(size):
                    owner = flipped(me, distances_of(order, slot))
                    work[part][slot] = terms_ref[owner, :, columns]
            else:
                copies[part].wait()
                for slot in range(2 * count):
                    work[part][slot] = (
                        work[part][slot].astype(F32) + came[part][2 * count + slot].astype(F32)
                    ).astype(BF16)
            copies[part] = pltpu.make_async_remote_copy(
                src_ref=work[part].at[count : 2 * count],
                dst_ref=came[part].at[count : 2 * count],
                send_sem=send_sem.at[part, step],
                recv_sem=recv_sem.at[part, step],
                device_id={"dp": flipped(me, [order[step]])},
                device_id_type=MESH,
            )
            copies[part].start()
    for part, (columns, _) in enumerate(parts):
        copies[part].wait()
        total_ref[:, columns] = (work[part][0].astype(F32) + came[part][1].astype(F32)) * scale


def modulate_kernel(images_ref, styles_ref, modulated_ref):
    modulated_ref[0] = (images_ref[0].T.astype(F32) * styles_ref[0]).astype(BF16)


def finish_kernel(after_ref, images_ref, styles_ref, *rest):
    del after_ref
    parts, (input_ref, style_ref) = rest[:-2], rest[-2:]
    total = 0.0
    for part in parts:
        total = total + part[0].astype(F32)
    input_ref[0] = (total * styles_ref[0]).astype(BF16)
    style = jnp.sum(total * images_ref[0].astype(F32), axis=1, keepdims=True)
    style_ref[0] = jnp.broadcast_to(style, (style.shape[0], LANES)).T[:1, :]


def exchange_scratch(size, parts, rows, buffers):
    steps = len(parts[0][1])
    return [pltpu.SemaphoreType.DMA((len(parts), steps))] * 2 + [
        pltpu.VMEM((size, rows, columns.stop - columns.start), BF16) for columns, _ in parts
    ] * buffers


def gather_rows(mine, after, size):
    rows, columns = mine.shape
    parts = orders(size, columns)
    vmem = pl.BlockSpec(memory_space=pltpu.VMEM)
    return pl.pallas_call(
        functools.partial(gather_kernel, size, parts, TAPS),
        out_shape=[
            jax.ShapeDtypeStruct((size, rows, columns), BF16),
            jax.ShapeDtypeStruct((size, rows, columns // TAPS), F32),
        ],
        in_specs=[vmem, pl.BlockSpec(memory_space=pl.ANY)],
        out_specs=[vmem, vmem],
        scratch_shapes=exchange_scratch(size, parts, rows, 1),
        compiler_params=pltpu.CompilerParams(collective_id=0, has_side_effects=True, vmem_limit_bytes=VMEM),
        name="gather",
    )(mine, after)


def reduce_rows(terms, size, scale):
    _, rows, columns = terms.shape
    parts = orders(size, columns)
    vmem = pl.BlockSpec(memory_space=pltpu.VMEM)
    return pl.pallas_call(
        functools.partial(reduce_kernel, size, parts, scale),
        out_shape=jax.ShapeDtypeStruct((rows, columns), F32),
        in_specs=[vmem],
        out_specs=vmem,
        scratch_shapes=exchange_scratch(size, parts, rows, 2),
        compiler_params=pltpu.CompilerParams(collective_id=1, has_side_effects=True, vmem_limit_bytes=VMEM),
        name="reduce",
    )(terms)


def on_device(n, images, styles, weight, cotangent):
    batch, block, pixels = images.shape
    outputs = weight.shape[1]
    inputs = styles.shape[1]
    side = math.isqrt(pixels)
    me = lax.axis_index("cout")
    position = me.reshape(1).astype(jnp.int32)

    def send(values, step):
        return lax.ppermute(values, "cout", [(j, (j + step) % n) for j in range(n)])

    local_styles = lax.dynamic_slice_in_dim(styles, me * block, block, 1)
    vmem = pl.BlockSpec(memory_space=pltpu.VMEM)
    plan = pltpu.CompilerParams(vmem_limit_bytes=VMEM)
    one_image = pl.BlockSpec((1, block, pixels), lambda i: (i, 0, 0))
    modulated = pl.pallas_call(
        modulate_kernel,
        grid=(batch,),
        out_shape=jax.ShapeDtypeStruct((batch, pixels, block), BF16),
        in_specs=[one_image, pl.BlockSpec((1, 1, block), lambda i: (i, 0, 0))],
        out_specs=pl.BlockSpec((1, pixels, block), lambda i: (i, 0, 0)),
        compiler_params=plan,
        name="modulate",
    )(images, local_styles[:, None, :])
    maps = [modulated] + [send(modulated, step) for step in range(1, n)]

    mine = weight.transpose(2, 0, 1).reshape(weight.shape[2], TAPS * outputs)
    size = lax.axis_size("dp")
    by_input, kernel_energy = gather_rows(mine, modulated, size)
    by_input = by_input.reshape(inputs, TAPS * outputs)
    kernel_energy = kernel_energy.reshape(inputs, outputs)
    style_square = styles * styles
    energy = jnp.dot(style_square, kernel_energy, precision=HIGHEST)
    demodulation = lax.rsqrt(energy + epsilon)
    factor = demodulation[:, :, None]

    smem = pl.BlockSpec(memory_space=pltpu.SMEM)
    work = 2 * TAPS * inputs * outputs * pixels
    one = lambda i: (i, 0, 0)
    whole = lambda i: (0, 0)
    parts = pl.pallas_call(
        functools.partial(back_kernel, side, n),
        grid=(batch,),
        out_shape=[jax.ShapeDtypeStruct((batch, block, pixels), BF16)] * n,
        in_specs=[
            smem,
            pl.BlockSpec((1, outputs, pixels), one),
            pl.BlockSpec((1, outputs, 1), one),
            pl.BlockSpec(by_input.shape, whole),
        ],
        out_specs=[pl.BlockSpec((1, block, pixels), one)] * n,
        scratch_shapes=[
            pltpu.VMEM((pixels + 2 * side, 3 * outputs), BF16),
            pltpu.VMEM((TAPS * outputs, inputs), BF16),
            pltpu.VMEM((inputs, pixels), BF16),
        ],
        compiler_params=plan,
        cost_estimate=pl.CostEstimate(
            flops=batch * work, bytes_accessed=8 * batch * outputs * pixels, transcendentals=0
        ),
        name="back",
    )(position, cotangent, factor, by_input)
    backs = [send(part, step) if step else part for step, part in enumerate(parts)]

    lanes = -(-batch // LANES) * LANES
    squares = jnp.pad(style_square.T, ((0, 0), (0, lanes - batch)))
    output, energy_columns, gradient = pl.pallas_call(
        functools.partial(forward_kernel, side, n),
        grid=(batch,),
        out_shape=[
            jax.ShapeDtypeStruct((batch, outputs, pixels), BF16),
            jax.ShapeDtypeStruct((outputs, lanes), F32),
            jax.ShapeDtypeStruct((inputs, TAPS * outputs), BF16),
        ],
        in_specs=[
            smem,
            pl.BlockSpec((1, outputs, pixels), one),
            pl.BlockSpec((1, outputs, 1), one),
            pl.BlockSpec(squares.shape, whole),
            pl.BlockSpec(by_input.shape, whole),
        ]
        + [pl.BlockSpec((1, pixels, block), one)] * n,
        out_specs=[
            pl.BlockSpec((1, outputs, pixels), one),
            pl.BlockSpec((outputs, lanes), whole),
            pl.BlockSpec((inputs, TAPS * outputs), whole),
        ],
        scratch_shapes=[
            pltpu.VMEM((pixels + 2 * side, 3 * inputs), BF16),
            pltpu.VMEM((TAPS * inputs, outputs), BF16),
            pltpu.VMEM((inputs, outputs), F32),
            pltpu.VMEM((outputs, TAPS * inputs), F32),
        ],
        compiler_params=pltpu.CompilerParams(vmem_limit_bytes=VMEM),
        cost_estimate=pl.CostEstimate(
            flops=2 * batch * work, bytes_accessed=16 * batch * outputs * pixels, transcendentals=0
        ),
        name="forward",
    )(position, cotangent, factor, squares, by_input, *maps)

    gradient = gradient.reshape(size, inputs // size, TAPS * outputs)
    gradient = reduce_rows(gradient, size, 1.0 / (batch * size))
    weight_grad = gradient.reshape(-1, TAPS, outputs).transpose(1, 2, 0)

    energy_grad = energy_columns[:, :batch].T
    style_terms = 2.0 * styles * jnp.dot(energy_grad, kernel_energy.T, precision=HIGHEST)
    style_terms = style_terms.astype(BF16)
    style_sum = 0.0
    for step in range(n):
        part = lax.dynamic_slice_in_dim(style_terms, lax.rem(me + step, n) * block, block, 1)
        style_sum = style_sum + (send(part, step) if step else part).astype(F32)

    input_grad, style_part = pl.pallas_call(
        finish_kernel,
        grid=(batch,),
        out_shape=[
            jax.ShapeDtypeStruct(images.shape, BF16),
            jax.ShapeDtypeStruct((batch, 1, block), F32),
        ],
        in_specs=[pl.BlockSpec(memory_space=pl.ANY), one_image, pl.BlockSpec((1, block, 1), one)]
        + [one_image] * n,
        out_specs=[one_image, pl.BlockSpec((1, 1, block), one)],
        compiler_params=plan,
        name="finish",
    )(gradient, images, local_styles[:, :, None], *backs)
    style_grad = style_part[:, 0, :] + style_sum
    return (output, input_grad, style_grad, weight_grad)


def solution(mesh):
    return jax.shard_map(
        functools.partial(on_device, mesh.shape["cout"]),
        mesh=mesh,
        in_specs=(
            P("dp", "cout", None),
            P("dp", None),
            P(None, "cout", "dp"),
            P("dp", "cout", None),
        ),
        out_specs=(
            P("dp", "cout", None),
            P("dp", "cout", None),
            P("dp", "cout"),
            P(None, "cout", "dp"),
        ),
        check_vma=False,
    )
```

```python
import functools
import math

import jax
import jax.numpy as jnp
from jax import lax
from jax.experimental import pallas as pl
from jax.experimental.pallas import tpu as pltpu
from jax.sharding import PartitionSpec as P

epsilon = 1e-08
TAPS = 9
BF16 = jnp.bfloat16
F32 = jnp.float32
HIGHEST = lax.Precision.HIGHEST
LANES = 128
VMEM = 56 * 2**20
MESH = pl.DeviceIdType.MESH


def spread(columns, at, lane, stride, values, side):
    rows, width = values.shape
    column = lax.broadcasted_iota(jnp.int32, values.shape, 0) % side
    for group, moved in enumerate(
        (
            jnp.where(column >= 1, pltpu.roll(values, 1, 0), 0.0),
            values,
            jnp.where(column < side - 1, pltpu.roll(values, rows - 1, 0), 0.0),
        )
    ):
        start = group * stride + lane
        columns[side + at : side + at + rows, start : start + width] = moved.astype(BF16)


def clear_margins(columns, side):
    margin = jnp.zeros((side, columns.shape[1]), BF16)
    columns[:side, :] = margin
    columns[columns.shape[0] - side :, :] = margin


def convolve(columns, weights, pixels, side):
    depth = columns.shape[1]
    total = 0.0
    for row in range(3):
        total = total + jnp.dot(
            columns[row * side : row * side + pixels, :],
            weights[row * depth : (row + 1) * depth, :],
            preferred_element_type=F32,
        )
    return total


def back_kernel(side, n, me_ref, upstream_ref, factor_ref, weight_ref, *rest):
    out_refs, columns, turned, terms = rest[:n], rest[n], rest[n + 1], rest[n + 2]
    outputs, pixels = upstream_ref.shape[1:]
    block = weight_ref.shape[0] // n

    @pl.when(pl.program_id(0) == 0)
    def _():
        clear_margins(columns, side)
        for tap in range(TAPS):
            mirror = TAPS - 1 - tap
            turned[mirror * outputs : (mirror + 1) * outputs, :] = weight_ref[
                :, tap * outputs : (tap + 1) * outputs
            ].T

    for at in range(0, pixels, LANES):
        scaled = upstream_ref[0, :, at : at + LANES].astype(F32) * factor_ref[0]
        spread(columns, at, 0, outputs, scaled.T, side)
    terms[...] = convolve(columns, turned, pixels, side).astype(BF16).T
    for step in range(n):
        owner = lax.rem(me_ref[0] + step, n)
        out_refs[step][0] = terms[pl.ds(pl.multiple_of(owner * block, block), block), :]


def forward_kernel(side, n, me_ref, upstream_ref, factor_ref, squares_ref, weight_ref, *rest):
    maps = rest[:n]
    output_ref, energy_ref, gradient_ref, columns, forward_ref, radial_ref, total = rest[n:]
    outputs, pixels = upstream_ref.shape[1:]
    block = maps[0].shape[2]
    inputs = n * block
    image = pl.program_id(0)

    def rows_of(step):
        owner = lax.rem(me_ref[0] + n - step, n)
        return pl.ds(pl.multiple_of(owner * block, block), block)

    @pl.when(image == 0)
    def _():
        clear_margins(columns, side)
        for tap in range(TAPS):
            for step in range(n):
                at = tap * inputs + step * block
                forward_ref[at : at + block, :] = weight_ref[rows_of(step), tap * outputs : (tap + 1) * outputs]
        total[...] = jnp.zeros_like(total)
        energy_ref[...] = jnp.zeros_like(energy_ref)

    for step in range(n):
        for at in range(0, pixels, LANES):
            spread(columns, at, step * block, inputs, maps[step][0, at : at + LANES, :].astype(F32), side)

    factor = factor_ref[0]
    convolved = convolve(columns, forward_ref, pixels, side).T
    output_ref[0] = (factor * convolved).astype(BF16)
    upstream = upstream_ref[0].astype(F32)
    norm_grad = jnp.sum(upstream * convolved, axis=1, keepdims=True)
    energy_grad = -0.5 * norm_grad * (factor * factor * factor)
    lane = lax.broadcasted_iota(jnp.int32, energy_ref.shape, 1)
    energy_ref[...] += jnp.where(lane == image, energy_grad, 0.0)

    scaled = (upstream * factor).astype(BF16)
    depth = 3 * inputs
    for row in range(3):
        total[:, row * depth : (row + 1) * depth] += jnp.dot(
            scaled, columns[row * side : row * side + pixels, :], preferred_element_type=F32
        )

    @pl.when(image == pl.num_programs(0) - 1)
    def _():
        radial_ref[...] = 2.0 * lax.dot_general(
            squares_ref[...],
            energy_ref[...],
            (((1,), (1,)), ((), ())),
            precision=HIGHEST,
            preferred_element_type=F32,
        )
        for tap in range(TAPS):
            part = slice(tap * outputs, (tap + 1) * outputs)
            for step in range(n):
                at = tap * inputs + step * block
                gradient_ref[rows_of(step), part] = (
                    total[:, at : at + block].T
                    + weight_ref[rows_of(step), part].astype(F32) * radial_ref[rows_of(step), :]
                ).astype(BF16)


def flipped(me, distances):
    place = me
    for distance in distances:
        place = place + distance * (1 - 2 * lax.rem(lax.div(me, distance), 2))
    return place


def orders(size, columns):
    distances = [1 << bit for bit in range(size.bit_length() - 1)][::-1]
    if columns % (TAPS * LANES) or size < 8:
        return [(slice(0, columns), distances)]
    width = columns // TAPS
    turned = distances[-2:-1] + distances[:-2] + distances[-1:]
    return [
        (slice(part * width, (part + 1) * width), (distances, turned, distances)[part % 3]) for part in range(TAPS)
    ]


def distances_of(order, slot):
    return [distance for bit, distance in enumerate(order) if (slot >> bit) & 1]


def taps_in(columns, outputs):
    first = columns.start // outputs
    count = (columns.stop - columns.start) // outputs
    return [(first + tap, tap * outputs, (tap + 1) * outputs) for tap in range(count)]


def greet(me, order):
    barrier = pltpu.get_barrier_semaphore()
    for distance in order:
        pl.semaphore_signal(barrier, inc=1, device_id={"dp": flipped(me, [distance])}, device_id_type=MESH)
    pl.semaphore_wait(barrier, len(order))


def gather_kernel(size, parts, taps, mine_ref, after_ref, whole_ref, energy_ref, send_sem, recv_sem, *held):
    me = lax.axis_index("dp")
    del after_ref
    steps = len(parts[0][1])
    for part, (columns, _) in enumerate(parts):
        for tap, start, stop in taps_in(columns, mine_ref.shape[2]):
            held[part][0, :, start:stop] = mine_ref[tap]
    greet(me, parts[0][1])
    copies = [None] * len(parts)
    for step in range(steps):
        for part, (_, order) in enumerate(parts):
            if step:
                copies[part].wait()
            count = 1 << step
            copies[part] = pltpu.make_async_remote_copy(
                src_ref=held[part].at[0:count],
                dst_ref=held[part].at[count : 2 * count],
                send_sem=send_sem.at[part, step],
                recv_sem=recv_sem.at[part, step],
                device_id={"dp": flipped(me, [order[step]])},
                device_id_type=MESH,
            )
            copies[part].start()
    for copy in copies:
        copy.wait()
    outputs = energy_ref.shape[2]
    for part, (columns, order) in enumerate(parts):
        for slot in range(size):
            owner = flipped(me, distances_of(order, slot))
            whole_ref[owner, :, columns] = held[part][slot]
    for slot in range(size):
        energy = None
        for tap in range(taps):
            value = whole_ref[slot, :, tap * outputs : (tap + 1) * outputs].astype(F32)
            energy = value * value if energy is None else energy + value * value
        energy_ref[slot] = energy


def reduce_kernel(size, parts, scale, terms_ref, total_ref, send_sem, recv_sem, *scratch):
    me = lax.axis_index("dp")
    steps = len(parts[0][1])
    work, came = scratch[: len(parts)], scratch[len(parts) :]
    greet(me, parts[0][1])
    copies = [None] * len(parts)
    for step in range(steps - 1, -1, -1):
        count = 1 << step
        for part, (columns, order) in enumerate(parts):
            if step == steps - 1:
                for slot in range(size):
                    owner = flipped(me, distances_of(order, slot))
                    work[part][slot] = terms_ref[owner, :, columns]
            else:
                copies[part].wait()
                for slot in range(2 * count):
                    work[part][slot] = (
                        work[part][slot].astype(F32) + came[part][2 * count + slot].astype(F32)
                    ).astype(BF16)
            copies[part] = pltpu.make_async_remote_copy(
                src_ref=work[part].at[count : 2 * count],
                dst_ref=came[part].at[count : 2 * count],
                send_sem=send_sem.at[part, step],
                recv_sem=recv_sem.at[part, step],
                device_id={"dp": flipped(me, [order[step]])},
                device_id_type=MESH,
            )
            copies[part].start()
    for part, (columns, _) in enumerate(parts):
        copies[part].wait()
        total = (work[part][0].astype(F32) + came[part][1].astype(F32)) * scale
        for tap, start, stop in taps_in(columns, total_ref.shape[2]):
            total_ref[tap] = total[:, start:stop]


def modulate_kernel(images_ref, styles_ref, modulated_ref):
    modulated_ref[0] = (images_ref[0].T.astype(F32) * styles_ref[0]).astype(BF16)


def finish_kernel(after_ref, images_ref, styles_ref, *rest):
    del after_ref
    parts, (input_ref, style_ref) = rest[:-2], rest[-2:]
    total = 0.0
    for part in parts:
        total = total + part[0].astype(F32)
    styles = jnp.broadcast_to(styles_ref[0], (LANES, styles_ref.shape[2])).T[:, :1]
    input_ref[0] = (total * styles).astype(BF16)
    style = jnp.sum(total * images_ref[0].astype(F32), axis=1, keepdims=True)
    style_ref[0] = jnp.broadcast_to(style, (style.shape[0], LANES)).T[:1, :]


def exchange_scratch(size, parts, rows, buffers):
    steps = len(parts[0][1])
    return [pltpu.SemaphoreType.DMA((len(parts), steps))] * 2 + [
        pltpu.VMEM((size, rows, columns.stop - columns.start), BF16) for columns, _ in parts
    ] * buffers


def gather_rows(mine, after, size):
    taps, rows, outputs = mine.shape
    columns = taps * outputs
    parts = orders(size, columns)
    vmem = pl.BlockSpec(memory_space=pltpu.VMEM)
    return pl.pallas_call(
        functools.partial(gather_kernel, size, parts, TAPS),
        out_shape=[
            jax.ShapeDtypeStruct((size, rows, columns), BF16),
            jax.ShapeDtypeStruct((size, rows, columns // TAPS), F32),
        ],
        in_specs=[vmem, pl.BlockSpec(memory_space=pl.ANY)],
        out_specs=[vmem, vmem],
        scratch_shapes=exchange_scratch(size, parts, rows, 1),
        compiler_params=pltpu.CompilerParams(collective_id=0, has_side_effects=True, vmem_limit_bytes=VMEM),
        name="gather",
    )(mine, after)


def reduce_rows(terms, size, scale):
    _, rows, columns = terms.shape
    parts = orders(size, columns)
    vmem = pl.BlockSpec(memory_space=pltpu.VMEM)
    return pl.pallas_call(
        functools.partial(reduce_kernel, size, parts, scale),
        out_shape=jax.ShapeDtypeStruct((TAPS, rows, columns // TAPS), F32),
        in_specs=[vmem],
        out_specs=vmem,
        scratch_shapes=exchange_scratch(size, parts, rows, 2),
        compiler_params=pltpu.CompilerParams(collective_id=1, has_side_effects=True, vmem_limit_bytes=VMEM),
        name="reduce",
    )(terms)


def on_device(n, images, styles, weight, cotangent):
    batch, block, pixels = images.shape
    outputs = weight.shape[1]
    inputs = styles.shape[1]
    side = math.isqrt(pixels)
    me = lax.axis_index("cout")
    position = me.reshape(1).astype(jnp.int32)

    def send(values, step):
        return lax.ppermute(values, "cout", [(j, (j + step) % n) for j in range(n)])

    local_styles = lax.dynamic_slice_in_dim(styles, me * block, block, 1)
    vmem = pl.BlockSpec(memory_space=pltpu.VMEM)
    plan = pltpu.CompilerParams(vmem_limit_bytes=VMEM)
    one_image = pl.BlockSpec((1, block, pixels), lambda i: (i, 0, 0))
    modulated = pl.pallas_call(
        modulate_kernel,
        grid=(batch,),
        out_shape=jax.ShapeDtypeStruct((batch, pixels, block), BF16),
        in_specs=[one_image, pl.BlockSpec((1, 1, block), lambda i: (i, 0, 0))],
        out_specs=pl.BlockSpec((1, pixels, block), lambda i: (i, 0, 0)),
        compiler_params=plan,
        name="modulate",
    )(images, local_styles[:, None, :])
    maps = [modulated] + [send(modulated, step) for step in range(1, n)]

    mine = weight.transpose(0, 2, 1)
    size = lax.axis_size("dp")
    by_input, kernel_energy = gather_rows(mine, modulated, size)
    by_input = by_input.reshape(inputs, TAPS * outputs)
    kernel_energy = kernel_energy.reshape(inputs, outputs)
    style_square = styles * styles
    energy = jnp.dot(style_square, kernel_energy, precision=HIGHEST)
    demodulation = lax.rsqrt(energy + epsilon)
    factor = demodulation[:, :, None]

    smem = pl.BlockSpec(memory_space=pltpu.SMEM)
    work = 2 * TAPS * inputs * outputs * pixels
    one = lambda i: (i, 0, 0)
    whole = lambda i: (0, 0)
    parts = pl.pallas_call(
        functools.partial(back_kernel, side, n),
        grid=(batch,),
        out_shape=[jax.ShapeDtypeStruct((batch, block, pixels), BF16)] * n,
        in_specs=[
            smem,
            pl.BlockSpec((1, outputs, pixels), one),
            pl.BlockSpec((1, outputs, 1), one),
            pl.BlockSpec(by_input.shape, whole),
        ],
        out_specs=[pl.BlockSpec((1, block, pixels), one)] * n,
        scratch_shapes=[
            pltpu.VMEM((pixels + 2 * side, 3 * outputs), BF16),
            pltpu.VMEM((TAPS * outputs, inputs), BF16),
            pltpu.VMEM((inputs, pixels), BF16),
        ],
        compiler_params=plan,
        cost_estimate=pl.CostEstimate(
            flops=batch * work, bytes_accessed=8 * batch * outputs * pixels, transcendentals=0
        ),
        name="back",
    )(position, cotangent, factor, by_input)
    backs = [send(part, step) if step else part for step, part in enumerate(parts)]

    lanes = -(-batch // LANES) * LANES
    squares = jnp.pad(style_square.T, ((0, 0), (0, lanes - batch)))
    output, energy_columns, gradient = pl.pallas_call(
        functools.partial(forward_kernel, side, n),
        grid=(batch,),
        out_shape=[
            jax.ShapeDtypeStruct((batch, outputs, pixels), BF16),
            jax.ShapeDtypeStruct((outputs, lanes), F32),
            jax.ShapeDtypeStruct((inputs, TAPS * outputs), BF16),
        ],
        in_specs=[
            smem,
            pl.BlockSpec((1, outputs, pixels), one),
            pl.BlockSpec((1, outputs, 1), one),
            pl.BlockSpec(squares.shape, whole),
            pl.BlockSpec(by_input.shape, whole),
        ]
        + [pl.BlockSpec((1, pixels, block), one)] * n,
        out_specs=[
            pl.BlockSpec((1, outputs, pixels), one),
            pl.BlockSpec((outputs, lanes), whole),
            pl.BlockSpec((inputs, TAPS * outputs), whole),
        ],
        scratch_shapes=[
            pltpu.VMEM((pixels + 2 * side, 3 * inputs), BF16),
            pltpu.VMEM((TAPS * inputs, outputs), BF16),
            pltpu.VMEM((inputs, outputs), F32),
            pltpu.VMEM((outputs, TAPS * inputs), F32),
        ],
        compiler_params=pltpu.CompilerParams(vmem_limit_bytes=VMEM),
        cost_estimate=pl.CostEstimate(
            flops=2 * batch * work, bytes_accessed=16 * batch * outputs * pixels, transcendentals=0
        ),
        name="forward",
    )(position, cotangent, factor, squares, by_input, *maps)

    gradient = gradient.reshape(size, inputs // size, TAPS * outputs)
    gradient = reduce_rows(gradient, size, 1.0 / (batch * size))
    weight_grad = gradient.transpose(0, 2, 1)

    energy_grad = energy_columns[:, :batch].T
    style_terms = 2.0 * styles * jnp.dot(energy_grad, kernel_energy.T, precision=HIGHEST)
    style_terms = style_terms.astype(BF16)
    style_sum = 0.0
    for step in range(n):
        part = lax.dynamic_slice_in_dim(style_terms, lax.rem(me + step, n) * block, block, 1)
        style_sum = style_sum + (send(part, step) if step else part).astype(F32)

    input_grad, style_part = pl.pallas_call(
        finish_kernel,
        grid=(batch,),
        out_shape=[
            jax.ShapeDtypeStruct(images.shape, BF16),
            jax.ShapeDtypeStruct((batch, 1, block), F32),
        ],
        in_specs=[pl.BlockSpec(memory_space=pl.ANY), one_image, pl.BlockSpec((1, 1, block), one)]
        + [one_image] * n,
        out_specs=[one_image, pl.BlockSpec((1, 1, block), one)],
        compiler_params=plan,
        name="finish",
    )(gradient, images, local_styles[:, None, :], *backs)
    style_grad = style_part[:, 0, :] + style_sum
    return (output, input_grad, style_grad, weight_grad)


def solution(mesh):
    return jax.shard_map(
        functools.partial(on_device, mesh.shape["cout"]),
        mesh=mesh,
        in_specs=(
            P("dp", "cout", None),
            P("dp", None),
            P(None, "cout", "dp"),
            P("dp", "cout", None),
        ),
        out_specs=(
            P("dp", "cout", None),
            P("dp", "cout", None),
            P("dp", "cout"),
            P(None, "cout", "dp"),
        ),
        check_vma=False,
    )
```

```python
import functools
import math

import jax
import jax.numpy as jnp
from jax import lax
from jax.experimental import pallas as pl
from jax.experimental.pallas import tpu as pltpu
from jax.sharding import PartitionSpec as P

epsilon = 1e-08
TAPS = 9
BF16 = jnp.bfloat16
F32 = jnp.float32
HIGHEST = lax.Precision.HIGHEST
LANES = 128
VMEM = 56 * 2**20
MESH = pl.DeviceIdType.MESH


def spread(columns, at, lane, stride, values, side):
    rows, width = values.shape
    column = lax.broadcasted_iota(jnp.int32, values.shape, 0) % side
    for group, moved in enumerate(
        (
            jnp.where(column >= 1, pltpu.roll(values, 1, 0), 0.0),
            values,
            jnp.where(column < side - 1, pltpu.roll(values, rows - 1, 0), 0.0),
        )
    ):
        start = group * stride + lane
        columns[side + at : side + at + rows, start : start + width] = moved.astype(BF16)


def as_column(row):
    return jnp.broadcast_to(row, (LANES, row.shape[1])).T[:, :1]


def clear_margins(columns, side):
    margin = jnp.zeros((side, columns.shape[1]), BF16)
    columns[:side, :] = margin
    columns[columns.shape[0] - side :, :] = margin


def convolve(columns, weights, pixels, side):
    depth = columns.shape[1]
    total = 0.0
    for row in range(3):
        total = total + jnp.dot(
            columns[row * side : row * side + pixels, :],
            weights[row * depth : (row + 1) * depth, :],
            preferred_element_type=F32,
        )
    return total


def back_kernel(side, n, me_ref, upstream_ref, factor_ref, weight_ref, *rest):
    out_refs, columns, turned, terms = rest[:n], rest[n], rest[n + 1], rest[n + 2]
    outputs, pixels = upstream_ref.shape[1:]
    block = weight_ref.shape[0] // n

    @pl.when(pl.program_id(0) == 0)
    def _():
        clear_margins(columns, side)
        for tap in range(TAPS):
            mirror = TAPS - 1 - tap
            turned[mirror * outputs : (mirror + 1) * outputs, :] = weight_ref[
                :, tap * outputs : (tap + 1) * outputs
            ].T

    factor = as_column(factor_ref[0])
    for at in range(0, pixels, LANES):
        scaled = upstream_ref[0, :, at : at + LANES].astype(F32) * factor
        spread(columns, at, 0, outputs, scaled.T, side)
    terms[...] = convolve(columns, turned, pixels, side).astype(BF16).T
    for step in range(n):
        owner = lax.rem(me_ref[0] + step, n)
        out_refs[step][0] = terms[pl.ds(pl.multiple_of(owner * block, block), block), :]


def forward_kernel(side, n, me_ref, upstream_ref, factor_ref, squares_ref, weight_ref, *rest):
    maps = rest[:n]
    output_ref, energy_ref, gradient_ref, columns, forward_ref, radial_ref, total = rest[n:]
    outputs, pixels = upstream_ref.shape[1:]
    block = maps[0].shape[2]
    inputs = n * block
    image = pl.program_id(0)

    def rows_of(step):
        owner = lax.rem(me_ref[0] + n - step, n)
        return pl.ds(pl.multiple_of(owner * block, block), block)

    @pl.when(image == 0)
    def _():
        clear_margins(columns, side)
        for tap in range(TAPS):
            for step in range(n):
                at = tap * inputs + step * block
                forward_ref[at : at + block, :] = weight_ref[rows_of(step), tap * outputs : (tap + 1) * outputs]
        total[...] = jnp.zeros_like(total)
        energy_ref[...] = jnp.zeros_like(energy_ref)

    for step in range(n):
        for at in range(0, pixels, LANES):
            spread(columns, at, step * block, inputs, maps[step][0, at : at + LANES, :].astype(F32), side)

    factor = as_column(factor_ref[0])
    convolved = convolve(columns, forward_ref, pixels, side).T
    output_ref[0] = (factor * convolved).astype(BF16)
    upstream = upstream_ref[0].astype(F32)
    norm_grad = jnp.sum(upstream * convolved, axis=1, keepdims=True)
    energy_grad = -0.5 * norm_grad * (factor * factor * factor)
    lane = lax.broadcasted_iota(jnp.int32, energy_ref.shape, 1)
    energy_ref[...] += jnp.where(lane == image, energy_grad, 0.0)

    scaled = (upstream * factor).astype(BF16)
    depth = 3 * inputs
    for row in range(3):
        total[:, row * depth : (row + 1) * depth] += jnp.dot(
            scaled, columns[row * side : row * side + pixels, :], preferred_element_type=F32
        )

    @pl.when(image == pl.num_programs(0) - 1)
    def _():
        radial_ref[...] = 2.0 * lax.dot_general(
            squares_ref[...],
            energy_ref[...],
            (((1,), (1,)), ((), ())),
            precision=HIGHEST,
            preferred_element_type=F32,
        )
        for tap in range(TAPS):
            part = slice(tap * outputs, (tap + 1) * outputs)
            for step in range(n):
                at = tap * inputs + step * block
                gradient_ref[rows_of(step), part] = (
                    total[:, at : at + block].T
                    + weight_ref[rows_of(step), part].astype(F32) * radial_ref[rows_of(step), :]
                ).astype(BF16)


def flipped(me, distances):
    place = me
    for distance in distances:
        place = place + distance * (1 - 2 * lax.rem(lax.div(me, distance), 2))
    return place


def orders(size, columns):
    distances = [1 << bit for bit in range(size.bit_length() - 1)][::-1]
    if columns % (TAPS * LANES) or size < 8:
        return [(slice(0, columns), distances)]
    width = columns // TAPS
    turned = distances[-2:-1] + distances[:-2] + distances[-1:]
    return [
        (slice(part * width, (part + 1) * width), (distances, turned, distances)[part % 3]) for part in range(TAPS)
    ]


def distances_of(order, slot):
    return [distance for bit, distance in enumerate(order) if (slot >> bit) & 1]


def taps_in(columns, outputs):
    first = columns.start // outputs
    count = (columns.stop - columns.start) // outputs
    return [(first + tap, tap * outputs, (tap + 1) * outputs) for tap in range(count)]


def greet(me, order):
    barrier = pltpu.get_barrier_semaphore()
    for distance in order:
        pl.semaphore_signal(barrier, inc=1, device_id={"dp": flipped(me, [distance])}, device_id_type=MESH)
    pl.semaphore_wait(barrier, len(order))


def gather_kernel(size, parts, taps, mine_ref, after_ref, whole_ref, energy_ref, send_sem, recv_sem, *held):
    me = lax.axis_index("dp")
    del after_ref
    steps = len(parts[0][1])
    for part, (columns, _) in enumerate(parts):
        for tap, start, stop in taps_in(columns, mine_ref.shape[2]):
            held[part][0, :, start:stop] = mine_ref[tap]
    greet(me, parts[0][1])
    copies = [None] * len(parts)
    for step in range(steps):
        for part, (_, order) in enumerate(parts):
            if step:
                copies[part].wait()
            count = 1 << step
            copies[part] = pltpu.make_async_remote_copy(
                src_ref=held[part].at[0:count],
                dst_ref=held[part].at[count : 2 * count],
                send_sem=send_sem.at[part, step],
                recv_sem=recv_sem.at[part, step],
                device_id={"dp": flipped(me, [order[step]])},
                device_id_type=MESH,
            )
            copies[part].start()
    for copy in copies:
        copy.wait()
    outputs = energy_ref.shape[2]
    for part, (columns, order) in enumerate(parts):
        for slot in range(size):
            owner = flipped(me, distances_of(order, slot))
            whole_ref[owner, :, columns] = held[part][slot]
    for slot in range(size):
        energy = None
        for tap in range(taps):
            value = whole_ref[slot, :, tap * outputs : (tap + 1) * outputs].astype(F32)
            energy = value * value if energy is None else energy + value * value
        energy_ref[slot] = energy


def reduce_kernel(size, parts, scale, terms_ref, total_ref, send_sem, recv_sem, *scratch):
    me = lax.axis_index("dp")
    steps = len(parts[0][1])
    work, came = scratch[: len(parts)], scratch[len(parts) :]
    greet(me, parts[0][1])
    copies = [None] * len(parts)
    for step in range(steps - 1, -1, -1):
        count = 1 << step
        for part, (columns, order) in enumerate(parts):
            if step == steps - 1:
                for slot in range(size):
                    owner = flipped(me, distances_of(order, slot))
                    work[part][slot] = terms_ref[owner, :, columns]
            else:
                copies[part].wait()
                for slot in range(2 * count):
                    work[part][slot] = (
                        work[part][slot].astype(F32) + came[part][2 * count + slot].astype(F32)
                    ).astype(BF16)
            copies[part] = pltpu.make_async_remote_copy(
                src_ref=work[part].at[count : 2 * count],
                dst_ref=came[part].at[count : 2 * count],
                send_sem=send_sem.at[part, step],
                recv_sem=recv_sem.at[part, step],
                device_id={"dp": flipped(me, [order[step]])},
                device_id_type=MESH,
            )
            copies[part].start()
    for part, (columns, _) in enumerate(parts):
        copies[part].wait()
        total = (work[part][0].astype(F32) + came[part][1].astype(F32)) * scale
        for tap, start, stop in taps_in(columns, total_ref.shape[2]):
            total_ref[tap] = total[:, start:stop]


def modulate_kernel(images_ref, styles_ref, modulated_ref):
    modulated_ref[0] = (images_ref[0].T.astype(F32) * styles_ref[0]).astype(BF16)


def finish_kernel(after_ref, images_ref, styles_ref, *rest):
    del after_ref
    parts, (input_ref, style_ref) = rest[:-2], rest[-2:]
    total = 0.0
    for part in parts:
        total = total + part[0].astype(F32)
    styles = as_column(styles_ref[0])
    input_ref[0] = (total * styles).astype(BF16)
    style = jnp.sum(total * images_ref[0].astype(F32), axis=1, keepdims=True)
    style_ref[0] = jnp.broadcast_to(style, (style.shape[0], LANES)).T[:1, :]


def exchange_scratch(size, parts, rows, buffers):
    steps = len(parts[0][1])
    return [pltpu.SemaphoreType.DMA((len(parts), steps))] * 2 + [
        pltpu.VMEM((size, rows, columns.stop - columns.start), BF16) for columns, _ in parts
    ] * buffers


def gather_rows(mine, after, size):
    taps, rows, outputs = mine.shape
    columns = taps * outputs
    parts = orders(size, columns)
    vmem = pl.BlockSpec(memory_space=pltpu.VMEM)
    return pl.pallas_call(
        functools.partial(gather_kernel, size, parts, TAPS),
        out_shape=[
            jax.ShapeDtypeStruct((size, rows, columns), BF16),
            jax.ShapeDtypeStruct((size, rows, columns // TAPS), F32),
        ],
        in_specs=[vmem, pl.BlockSpec(memory_space=pl.ANY)],
        out_specs=[vmem, vmem],
        scratch_shapes=exchange_scratch(size, parts, rows, 1),
        compiler_params=pltpu.CompilerParams(collective_id=0, has_side_effects=True, vmem_limit_bytes=VMEM),
        name="gather",
    )(mine, after)


def reduce_rows(terms, size, scale):
    _, rows, columns = terms.shape
    parts = orders(size, columns)
    vmem = pl.BlockSpec(memory_space=pltpu.VMEM)
    return pl.pallas_call(
        functools.partial(reduce_kernel, size, parts, scale),
        out_shape=jax.ShapeDtypeStruct((TAPS, rows, columns // TAPS), F32),
        in_specs=[vmem],
        out_specs=vmem,
        scratch_shapes=exchange_scratch(size, parts, rows, 2),
        compiler_params=pltpu.CompilerParams(collective_id=1, has_side_effects=True, vmem_limit_bytes=VMEM),
        name="reduce",
    )(terms)


def on_device(n, images, styles, weight, cotangent):
    batch, block, pixels = images.shape
    outputs = weight.shape[1]
    inputs = styles.shape[1]
    side = math.isqrt(pixels)
    me = lax.axis_index("cout")
    position = me.reshape(1).astype(jnp.int32)

    def send(values, step):
        return lax.ppermute(values, "cout", [(j, (j + step) % n) for j in range(n)])

    local_styles = lax.dynamic_slice_in_dim(styles, me * block, block, 1)
    vmem = pl.BlockSpec(memory_space=pltpu.VMEM)
    plan = pltpu.CompilerParams(vmem_limit_bytes=VMEM)
    one_image = pl.BlockSpec((1, block, pixels), lambda i: (i, 0, 0))
    modulated = pl.pallas_call(
        modulate_kernel,
        grid=(batch,),
        out_shape=jax.ShapeDtypeStruct((batch, pixels, block), BF16),
        in_specs=[one_image, pl.BlockSpec((1, 1, block), lambda i: (i, 0, 0))],
        out_specs=pl.BlockSpec((1, pixels, block), lambda i: (i, 0, 0)),
        compiler_params=plan,
        name="modulate",
    )(images, local_styles[:, None, :])
    maps = [modulated] + [send(modulated, step) for step in range(1, n)]

    mine = weight.transpose(0, 2, 1)
    size = lax.axis_size("dp")
    by_input, kernel_energy = gather_rows(mine, modulated, size)
    by_input = by_input.reshape(inputs, TAPS * outputs)
    kernel_energy = kernel_energy.reshape(inputs, outputs)
    style_square = styles * styles
    energy = jnp.dot(style_square, kernel_energy, precision=HIGHEST)
    demodulation = lax.rsqrt(energy + epsilon)
    factor = demodulation[:, None, :]

    smem = pl.BlockSpec(memory_space=pltpu.SMEM)
    work = 2 * TAPS * inputs * outputs * pixels
    one = lambda i: (i, 0, 0)
    whole = lambda i: (0, 0)
    parts = pl.pallas_call(
        functools.partial(back_kernel, side, n),
        grid=(batch,),
        out_shape=[jax.ShapeDtypeStruct((batch, block, pixels), BF16)] * n,
        in_specs=[
            smem,
            pl.BlockSpec((1, outputs, pixels), one),
            pl.BlockSpec((1, 1, outputs), one),
            pl.BlockSpec(by_input.shape, whole),
        ],
        out_specs=[pl.BlockSpec((1, block, pixels), one)] * n,
        scratch_shapes=[
            pltpu.VMEM((pixels + 2 * side, 3 * outputs), BF16),
            pltpu.VMEM((TAPS * outputs, inputs), BF16),
            pltpu.VMEM((inputs, pixels), BF16),
        ],
        compiler_params=plan,
        cost_estimate=pl.CostEstimate(
            flops=batch * work, bytes_accessed=8 * batch * outputs * pixels, transcendentals=0
        ),
        name="back",
    )(position, cotangent, factor, by_input)
    backs = [send(part, step) if step else part for step, part in enumerate(parts)]

    lanes = -(-batch // LANES) * LANES
    squares = jnp.pad(style_square.T, ((0, 0), (0, lanes - batch)))
    output, energy_columns, gradient = pl.pallas_call(
        functools.partial(forward_kernel, side, n),
        grid=(batch,),
        out_shape=[
            jax.ShapeDtypeStruct((batch, outputs, pixels), BF16),
            jax.ShapeDtypeStruct((outputs, lanes), F32),
            jax.ShapeDtypeStruct((inputs, TAPS * outputs), BF16),
        ],
        in_specs=[
            smem,
            pl.BlockSpec((1, outputs, pixels), one),
            pl.BlockSpec((1, 1, outputs), one),
            pl.BlockSpec(squares.shape, whole),
            pl.BlockSpec(by_input.shape, whole),
        ]
        + [pl.BlockSpec((1, pixels, block), one)] * n,
        out_specs=[
            pl.BlockSpec((1, outputs, pixels), one),
            pl.BlockSpec((outputs, lanes), whole),
            pl.BlockSpec((inputs, TAPS * outputs), whole),
        ],
        scratch_shapes=[
            pltpu.VMEM((pixels + 2 * side, 3 * inputs), BF16),
            pltpu.VMEM((TAPS * inputs, outputs), BF16),
            pltpu.VMEM((inputs, outputs), F32),
            pltpu.VMEM((outputs, TAPS * inputs), F32),
        ],
        compiler_params=pltpu.CompilerParams(vmem_limit_bytes=VMEM),
        cost_estimate=pl.CostEstimate(
            flops=2 * batch * work, bytes_accessed=16 * batch * outputs * pixels, transcendentals=0
        ),
        name="forward",
    )(position, cotangent, factor, squares, by_input, *maps)

    gradient = gradient.reshape(size, inputs // size, TAPS * outputs)
    gradient = reduce_rows(gradient, size, 1.0 / (batch * size))
    weight_grad = gradient.transpose(0, 2, 1)

    energy_grad = energy_columns[:, :batch].T
    style_terms = 2.0 * styles * jnp.dot(energy_grad, kernel_energy.T, precision=HIGHEST)
    style_terms = style_terms.astype(BF16)
    style_sum = 0.0
    for step in range(n):
        part = lax.dynamic_slice_in_dim(style_terms, lax.rem(me + step, n) * block, block, 1)
        style_sum = style_sum + (send(part, step) if step else part).astype(F32)

    input_grad, style_part = pl.pallas_call(
        finish_kernel,
        grid=(batch,),
        out_shape=[
            jax.ShapeDtypeStruct(images.shape, BF16),
            jax.ShapeDtypeStruct((batch, 1, block), F32),
        ],
        in_specs=[pl.BlockSpec(memory_space=pl.ANY), one_image, pl.BlockSpec((1, 1, block), one)]
        + [one_image] * n,
        out_specs=[one_image, pl.BlockSpec((1, 1, block), one)],
        compiler_params=plan,
        name="finish",
    )(gradient, images, local_styles[:, None, :], *backs)
    style_grad = style_part[:, 0, :] + style_sum
    return (output, input_grad, style_grad, weight_grad)


def solution(mesh):
    return jax.shard_map(
        functools.partial(on_device, mesh.shape["cout"]),
        mesh=mesh,
        in_specs=(
            P("dp", "cout", None),
            P("dp", None),
            P(None, "cout", "dp"),
            P("dp", "cout", None),
        ),
        out_specs=(
            P("dp", "cout", None),
            P("dp", "cout", None),
            P("dp", "cout"),
            P(None, "cout", "dp"),
        ),
        check_vma=False,
    )
```
